128 devices in a mesh: dp: 16 (over z, y_lo, core), mp: 8 (over y_hi, x).
Axes of the slice: x: 4, y: 4 (y_hi: 2, y_lo: 2; y = y_hi * 2 + y_lo), z: 4, core: 2. Of those that a mesh axis runs over, the one named last changes fastest.
Arguments:
- out_grad: bfloat16 [16384, 4096], P(('dp', 'mp')), may hold values from -24 to 24
- gate_pre: bfloat16 [16384, 14336], P('dp', 'mp'), may hold values from -6 to 6
- up_pre: bfloat16 [16384, 14336], P('dp', 'mp'), may hold values from -6 to 6
- down_weight: bfloat16 [14336, 4096], P('mp', 'dp'), may hold values from -0.046875 to 0.046875
Outputs:
- grad_gate_pre: bfloat16 [16384, 14336], P('dp', 'mp')
- grad_up_pre: bfloat16 [16384, 14336], P('dp', 'mp')
- grad_down: bfloat16 [14336, 4096], P('mp', 'dp')
The draws below stay inside these ranges and needn't reach their ends.
All inputs are finite; a program needn't handle non-finite values.
Results may differ from the reference program's by a relative error of at most 0.022.
Values may be sent and summed in bfloat16 or wider, within the bound.
A program may use at most 128 MiB of HBM per device.

```python
import math
import jax
import jax.numpy as jnp
from jax import lax

D = 4096
FF = 14336
TOK_DEV = 128
TOKENS = 16384
N_DP = 16
N_MP = 8


def spiked(array, stream_key, source, target, shards_of, factor):
    def block_of(axis_at):
        return (jnp.arange(array.shape[axis_at]) // (array.shape[axis_at] // shards_of)).reshape((-1,) + (1,) * (array.ndim - 1 - axis_at))

    one_side = jax.random.permutation(stream_key, shards_of)[block_of(target)]
    second = (block_of(target) + shards_of // 2) % shards_of
    return jnp.where((block_of(source) == one_side) | (block_of(source) == second), factor * array, array)


def shard_levels(rng, shape, split, smallest, largest):
    def one(position, parts):
        steps = jax.random.uniform(jax.random.fold_in(jax.random.fold_in(rng, 6), position), (parts,), jnp.float32, smallest / len(split), largest / len(split))
        return jnp.repeat(jnp.exp(steps), shape[position] // parts).reshape((-1,) + (1,) * (len(shape) - position - 1))

    loudness = one(*split[0])
    for cut in split[1:]:
        loudness = loudness * one(*cut)
    return loudness


def gaussian(own_key, dims, deviation, most, split=(), dtype=jnp.bfloat16):
    result = jax.random.normal(own_key, dims, jnp.float32) * deviation
    if len(split) > 0:
        result = shard_levels(own_key, dims, split, -0.22, 0.18) * result
    return jnp.clip(result, min=-most, max=most).astype(dtype)


def bell_draw_with(stream_key, extent, spread, limit, cuts, heavy, kind=jnp.bfloat16):
    result = spread * jax.random.normal(stream_key, extent, jnp.float32)
    if cuts:
        result = result * shard_levels(stream_key, extent, cuts, -0.22, 0.18)
    return jnp.clip(spiked(result, jax.random.fold_in(stream_key, 3), *heavy), -limit, limit).astype(kind)


def setup_inputs(seed: int = 0) -> dict:
    streams_of = jax.random.split(jax.random.key(seed), 5)
    out_grad = bell_draw_with(streams_of[0], (TOKENS, D), 1.0, 24.0, ((0, 128),), (0, 1, 128, 5.5))
    gate_pre = gaussian(streams_of[1], (TOKENS, FF), 1.0, 6.0, ((0, 16), (1, 8)))
    up_pre = gaussian(streams_of[2], (TOKENS, FF), 1.0, 6.0, ((0, 16), (1, 8)))
    down_weight = gaussian(streams_of[3], (FF, D), FF ** -0.5, 0.046875, ((0, 8), (1, 16)))
    return {"out_grad": out_grad, "gate_pre": gate_pre, "up_pre": up_pre, "down_weight": down_weight}


def reference(out_grad, gate_pre, up_pre, down_weight):
    rows = TOK_DEV * N_MP
    grads = out_grad.reshape(N_DP, rows, D)
    gates = gate_pre.reshape(N_DP, rows, FF)
    ups = up_pre.reshape(N_DP, rows, FF)

    def replica_step(total, pieces):
        grad_rows, gate_rows, up_rows = pieces
        gate_float = gate_rows.astype(jnp.float32)
        up_float = up_rows.astype(jnp.float32)
        sigmoid_gate = jax.nn.sigmoid(gate_float)
        silu_gate = gate_float * sigmoid_gate
        hidden = (silu_gate * up_float).astype(jnp.bfloat16)
        d_hidden = jnp.dot(grad_rows, down_weight.T, preferred_element_type=jnp.float32)
        grad_gate = (d_hidden * up_float * sigmoid_gate * (1.0 + gate_float * (1.0 - sigmoid_gate))).astype(jnp.bfloat16)
        grad_up = (d_hidden * silu_gate).astype(jnp.bfloat16)
        term = jnp.dot(hidden.T, grad_rows, preferred_element_type=jnp.float32)
        term = lax.optimization_barrier(term.astype(jnp.bfloat16)).astype(jnp.float32)
        return (total + term, (grad_gate, grad_up))
    total, (grad_gate, grad_up) = lax.scan(replica_step, jnp.zeros((FF, D), jnp.float32), (grads, gates, ups))
    grad_down = (total * (1.0 / math.sqrt(TOKENS))).astype(jnp.bfloat16)
    return (grad_gate.reshape(TOKENS, FF), grad_up.reshape(TOKENS, FF), grad_down)
```

```python
import math

import jax
import jax.numpy as jnp
from jax import lax
from jax.experimental import pallas as pl
from jax.experimental.pallas import tpu as pltpu
from jax.sharding import PartitionSpec as P

MESH = pl.DeviceIdType.MESH
F32 = jnp.float32
BF16 = jnp.bfloat16

ORDER = ((2, 1), (2, 0), (1, 1), (-1, 1), (1, 0), (-1, 0), (0, 1), (0, 0))
SLOT = {at: k for k, at in enumerate(ORDER)}
LAG = 2


def kernel(
    og, gp, up, w, gg, gu, gd,
    o_all, w_all, h_t, own, pre, snd, half_in, full_in, y_in, acc, gbuf, ubuf, ggbuf, gubuf,
    o_send, o_recv, w_send, w_recv, wc_send, wc_recv, t_send, t_recv, z_send, z_recv, y_send, y_recv,
    o_local, w_local, in_sem, out_sem, gd_sem,
):
    TB = og.shape[0]
    BLK = w.shape[1]
    FFD = w.shape[0]
    TOK = gp.shape[0]
    HALF = FFD // 2
    TH = TB // 2
    NT = FFD // BLK
    norm = 1.0 / math.sqrt(TOK * 16)

    dp = lax.axis_index("dp")
    mp = lax.axis_index("mp")
    z, yl, c = dp // 4, (dp // 2) % 2, dp % 2
    yh, x = mp // 4, mp % 4

    def dev(dz=0, o=0, cc=0, h=0, dx=0):
        a = ((z + dz + 4) % 4) * 4 + ((yl + o) % 2) * 2 + (c + cc) % 2
        b = ((yh + h) % 2) * 4 + (x + dx + 4) % 4
        return (a, b)

    ZP, ZM, YP, CP = dev(dz=1), dev(dz=-1), dev(o=1), dev(cc=1)
    HP, XP, XM = dev(h=1), dev(dx=1), dev(dx=-1)

    sends = []

    def send(src, dst, ss, rs, to):
        cp = pltpu.make_async_remote_copy(src, dst, ss, rs, device_id=to, device_id_type=MESH)
        cp.start()
        sends.append(cp)
        return cp

    def arrived(dst, ss, rs):
        pltpu.make_async_remote_copy(dst, dst, ss, rs, device_id=CP, device_id_type=MESH).wait_recv()

    barrier = pltpu.get_barrier_semaphore()
    for to in (ZP, ZM, YP, CP, HP, XP, XM):
        pl.semaphore_signal(barrier, inc=1, device_id=to, device_id_type=MESH)

    def tile_in(n, slot):
        cols = pl.ds(pl.multiple_of(n * BLK, BLK), BLK)
        return (
            pltpu.make_async_copy(gp.at[:, cols], gbuf.at[slot], in_sem.at[slot, 0]),
            pltpu.make_async_copy(up.at[:, cols], ubuf.at[slot], in_sem.at[slot, 1]),
        )

    def tile_out(n, slot):
        cols = pl.ds(pl.multiple_of(n * BLK, BLK), BLK)
        return (
            pltpu.make_async_copy(ggbuf.at[slot], gg.at[:, cols], out_sem.at[slot, 0]),
            pltpu.make_async_copy(gubuf.at[slot], gu.at[:, cols], out_sem.at[slot, 1]),
        )

    def o_cols(k):
        return pl.ds(k * 2 * BLK, 2 * BLK)

    def o_rows(h, dx, part=None):
        base = (((yh + h) % 2) * 4 + (x + dx + 4) % 4) * TB
        if part is None:
            return pl.ds(pl.multiple_of(base, TB), TB)
        return pl.ds(pl.multiple_of(base + part * TH, TH), TH)

    def w_cols(k, cc):
        return pl.ds((2 * k + cc) * BLK, BLK)

    w_own = pltpu.make_async_copy(w, w_all.at[:, w_cols(SLOT[0, 0], 0)], w_local)
    w_own.start()
    o_own = []
    for k, (dz, o) in enumerate(ORDER):
        for cc in range(2):
            d = ((z + dz + 4) % 4) * 4 + ((yl + o) % 2) * 2 + (c + cc) % 2
            cp = pltpu.make_async_copy(
                og.at[:, pl.ds(pl.multiple_of(d * BLK, BLK), BLK)],
                o_all.at[o_rows(0, 0), pl.ds((2 * k + cc) * BLK, BLK)],
                o_local.at[k, cc],
            )
            cp.start()
            o_own.append(cp)
    for slot in range(2):
        for cp in tile_in(slot, slot):
            cp.start()

    pl.semaphore_wait(barrier, 7)

    def w_part(k, cc, part):
        return w_all.at[pl.ds(part * HALF, HALF), w_cols(k, cc)]

    def w_to(src, k, part, sem, to):
        send(src, w_part(k, 0, part), w_send.at[sem], w_recv.at[k, part], to)

    def w_got(k, part):
        arrived(w_part(k, 0, part), w_send.at[0], w_recv.at[k, part])

    def w_share(k):
        send(
            w_all.at[:, w_cols(k, 0)], w_all.at[:, w_cols(k, 1)], wc_send.at[k], wc_recv.at[k], CP
        )

    def W0():
        a, b = w.at[pl.ds(0, HALF), :], w.at[pl.ds(HALF, HALF), :]
        w_to(a, SLOT[-1, 0], 0, 0, ZP)
        w_to(b, SLOT[1, 0], 1, 1, ZM)
        w_to(a, SLOT[0, 1], 0, 2, YP)
        w_to(b, SLOT[-1, 0], 1, 3, ZP)
        w_to(a, SLOT[1, 0], 0, 4, ZM)
        w_to(b, SLOT[0, 1], 1, 5, YP)

    def W1(o):
        w_got(SLOT[-1, o], 0)
        w_to(w_part(SLOT[-1, o], 0, 0), SLOT[2, o], 0, 6 + 2 * o, ZP)
        w_got(SLOT[1, o], 1)
        w_to(w_part(SLOT[1, o], 0, 1), SLOT[2, o], 1, 7 + 2 * o, ZM)

    def W2():
        k = SLOT[0, 1]
        w_got(k, 0)
        w_to(w_part(k, 0, 0), SLOT[-1, 1], 0, 10, ZP)
        w_to(w_part(k, 0, 0), SLOT[1, 1], 0, 11, ZM)
        w_got(k, 1)
        w_to(w_part(k, 0, 1), SLOT[1, 1], 1, 12, ZM)
        w_to(w_part(k, 0, 1), SLOT[-1, 1], 1, 13, ZP)
        w_share(k)

    def W4(o):
        w_got(SLOT[-1, o], 1)
        w_share(SLOT[-1, o])
        w_got(SLOT[1, o], 0)
        w_share(SLOT[1, o])

    def W5(o):
        k = SLOT[2, o]
        w_got(k, 0)
        w_got(k, 1)
        w_share(k)

    def o_to(k, h, dx, part, kind, to):
        ref = o_all.at[o_rows(h, dx, part), o_cols(k)]
        send(ref, ref, o_send.at[k, kind], o_recv.at[k, kind], to)

    def o_got(k, h, dx, part, kind):
        ref = o_all.at[o_rows(h, dx, part), o_cols(k)]
        arrived(ref, o_send.at[k, kind], o_recv.at[k, kind])

    def O0(k):
        o_own[2 * k].wait()
        o_own[2 * k + 1].wait()
        o_to(k, 0, 0, None, 0, HP)
        o_to(k, 0, 0, None, 1, XP)
        o_to(k, 0, 0, None, 2, XM)

    def O1(k):
        o_got(k, 0, -1, None, 1)
        o_to(k, 0, -1, 0, 3, XP)
        o_got(k, 0, 1, None, 2)
        o_to(k, 0, 1, 1, 4, XM)
        o_got(k, 1, 0, None, 0)
        o_to(k, 1, 0, None, 5, XP)
        o_to(k, 1, 0, None, 6, XM)

    def O2(k):
        o_got(k, 1, -1, None, 5)
        o_to(k, 1, -1, 0, 7, XP)
        o_got(k, 1, 1, None, 6)
        o_to(k, 1, 1, 1, 8, XM)

    def O3(k):
        o_got(k, 0, 2, 0, 3)
        o_got(k, 0, 2, 1, 4)
        o_got(k, 1, 2, 0, 7)
        o_got(k, 1, 2, 1, 8)

    def hidden_tile(n, _):
        slot = n % 2
        for cp in tile_in(n, slot):
            cp.wait()

        def rows(i, _):
            r = pl.ds(pl.multiple_of(i * 128, 128), 128)
            g = gbuf[slot, r, :].astype(F32)
            u = ubuf[slot, r, :].astype(F32)
            hid = g * jax.nn.sigmoid(g) * u
            h_t[pl.ds(pl.multiple_of(n * BLK, BLK), BLK), r] = hid.T.astype(BF16)
            return 0

        lax.fori_loop(0, TOK // 128, rows, 0)

        @pl.when(n + 2 < NT)
        def _():
            for cp in tile_in(n + 2, slot):
                cp.start()

        return 0

    def term(k, cc, dst):
        def rows(i, _):
            r = pl.ds(pl.multiple_of(i * HALF, HALF), HALF)
            dst[r, :] = jnp.dot(
                h_t[r, :], o_all[:, pl.ds((2 * k + cc) * BLK, BLK)], preferred_element_type=F32
            ).astype(BF16)
            return 0

        lax.fori_loop(0, 2, rows, 0)

    t_copies = {}

    def T(k):
        slot = k % 2
        if k >= 2:
            t_copies[k - 2].wait_send()
            sends[:] = [cp for cp in sends if cp is not t_copies[k - 2]]
        term(k, 1, snd.at[slot])
        t_copies[k] = send(snd.at[slot], pre.at[k], t_send.at[k], t_recv.at[k], CP)
        term(k, 0, own.at[k])

    def add(dst, others, start=0, size=None, scale=None):
        step = 128

        def rows(i, _):
            r = pl.ds(pl.multiple_of(start + i * step, step), step)
            total = dst[r, :].astype(F32)
            for ref, at in others:
                total += ref[pl.ds(pl.multiple_of(start - at + i * step, step), step), :].astype(F32)
            if scale is not None:
                total *= scale
            dst[r, :] = total.astype(BF16)
            return 0

        lax.fori_loop(0, size // step, rows, 0)

    def Pk(k):
        dz, o = ORDER[k]
        blk = own.at[k]
        arrived(pre.at[k], t_send.at[k], t_recv.at[k])
        up_half, down_half = pl.ds(0, HALF), pl.ds(HALF, HALF)
        if dz == 2:
            add(blk, [(pre.at[k], 0)], 0, FFD)
            send(blk.at[up_half, :], half_in.at[o, 0], z_send.at[o, 0], z_recv.at[o, 0], ZP)
            send(blk.at[down_half, :], half_in.at[o, 1], z_send.at[o, 1], z_recv.at[o, 1], ZM)
        elif dz == 1:
            add(blk, [(pre.at[k], 0)], HALF, HALF)
            arrived(half_in.at[o, 0], z_send.at[o, 0], z_recv.at[o, 0])
            add(blk, [(pre.at[k], 0), (half_in.at[o, 0], 0)], 0, HALF)
            send(blk, full_in.at[o, 0], z_send.at[o, 2], z_recv.at[o, 2], ZP)
        elif dz == -1:
            add(blk, [(pre.at[k], 0)], 0, HALF)
            arrived(half_in.at[o, 1], z_send.at[o, 1], z_recv.at[o, 1])
            add(blk, [(pre.at[k], 0), (half_in.at[o, 1], HALF)], HALF, HALF)
            send(blk, full_in.at[o, 1], z_send.at[o, 3], z_recv.at[o, 3], ZM)
        else:
            arrived(full_in.at[o, 0], z_send.at[o, 2], z_recv.at[o, 2])
            arrived(full_in.at[o, 1], z_send.at[o, 3], z_recv.at[o, 3])
            parts = [(pre.at[k], 0), (full_in.at[o, 0], 0), (full_in.at[o, 1], 0)]
            if o == 1:
                add(blk, parts, 0, FFD)
                send(blk, y_in, y_send, y_recv, YP)
            else:
                arrived(y_in, y_send, y_recv)
                add(blk, parts + [(y_in, 0)], 0, FFD, norm)
                cp = pltpu.make_async_copy(blk, gd, gd_sem)
                cp.start()
                cp.wait()

    def D(n, _):
        slot = n % 2

        def mm(i, _):
            r = pl.ds(pl.multiple_of(i * 512, 512), 512)
            acc[r, :] = lax.dot_general(
                o_all[r, :],
                w_all[pl.ds(pl.multiple_of(n * BLK, BLK), BLK), :],
                (((1,), (1,)), ((), ())),
                preferred_element_type=F32,
            )
            return 0

        lax.fori_loop(0, TOK // 512, mm, 0)
        for cp in tile_in(n, slot):
            cp.wait()

        @pl.when(n >= 2)
        def _():
            for cp in tile_out(n - 2, slot):
                cp.wait()

        def rows(i, _):
            r = pl.ds(pl.multiple_of(i * 64, 64), 64)
            g = gbuf[slot, r, :].astype(F32)
            u = ubuf[slot, r, :].astype(F32)
            d = acc[r, :]
            s = jax.nn.sigmoid(g)
            ggbuf[slot, r, :] = (d * u * s * (1.0 + g * (1.0 - s))).astype(BF16)
            gubuf[slot, r, :] = (d * (g * s)).astype(BF16)
            return 0

        lax.fori_loop(0, TOK // 64, rows, 0)
        for cp in tile_out(n, slot):
            cp.start()

        @pl.when(n + 2 < NT)
        def _():
            for cp in tile_in(n + 2, slot):
                cp.start()

        return 0

    W0()
    O0(0)
    O0(1)
    O0(2)
    lax.fori_loop(0, NT, hidden_tile, 0)
    for slot in range(2):
        for cp in tile_in(slot, slot):
            cp.start()
    w_own.wait()
    w_share(SLOT[0, 0])
    O1(0)
    W1(0)
    O1(1)
    O2(0)
    n_chunks = len(ORDER)
    for r in range(n_chunks):
        if r + 3 < n_chunks:
            O0(r + 3)
        if r + 2 < n_chunks:
            O1(r + 2)
        if r + 1 < n_chunks:
            O2(r + 1)
        if r == 1:
            W2()
        if r == 2:
            W4(0)
        if r == 4:
            W5(0)
        if r == 5:
            W1(1)
        if r == 6:
            W4(1)
        O3(r)
        T(r)
        if r - LAG >= 0:
            Pk(r - LAG)
    W5(1)
    for k in range(n_chunks):
        arrived(w_all.at[:, w_cols(k, 1)], wc_send.at[k], wc_recv.at[k])
    lax.fori_loop(0, 4, D, 0)
    Pk(6)
    lax.fori_loop(4, NT, D, 0)
    Pk(7)
    for cp in tile_out(NT - 2, (NT - 2) % 2) + tile_out(NT - 1, (NT - 1) % 2):
        cp.wait()
    for cp in sends:
        cp.wait_send()


def shards(out_grad, gate_pre, up_pre, down_weight):
    TB, D = out_grad.shape
    TOK, FFD = gate_pre.shape
    BLK = down_weight.shape[1]
    n = len(ORDER)
    any_spec = pl.BlockSpec(memory_space=pl.ANY)
    dma = pltpu.SemaphoreType.DMA
    flops = 4 * TOK * D * FFD
    return pl.pallas_call(
        kernel,
        out_shape=(
            jax.ShapeDtypeStruct((TOK, FFD), BF16),
            jax.ShapeDtypeStruct((TOK, FFD), BF16),
            jax.ShapeDtypeStruct((FFD, BLK), BF16),
        ),
        in_specs=[any_spec] * 4,
        out_specs=(any_spec,) * 3,
        scratch_shapes=[
            pltpu.VMEM((TOK, D), BF16),
            pltpu.VMEM((FFD, D), BF16),
            pltpu.VMEM((FFD, TOK), BF16),
            pltpu.VMEM((n, FFD, BLK), BF16),
            pltpu.VMEM((n, FFD, BLK), BF16),
            pltpu.VMEM((2, FFD, BLK), BF16),
            pltpu.VMEM((2, 2, FFD // 2, BLK), BF16),
            pltpu.VMEM((2, 2, FFD, BLK), BF16),
            pltpu.VMEM((FFD, BLK), BF16),
            pltpu.VMEM((TOK, BLK), F32),
            pltpu.VMEM((2, TOK, BLK), BF16),
            pltpu.VMEM((2, TOK, BLK), BF16),
            pltpu.VMEM((2, TOK, BLK), BF16),
            pltpu.VMEM((2, TOK, BLK), BF16),
            dma((n, 9)),
            dma((n, 9)),
            dma((14,)),
            dma((n, 2)),
            dma((n,)),
            dma((n,)),
            dma((n,)),
            dma((n,)),
            dma((2, 4)),
            dma((2, 4)),
            dma,
            dma,
            dma((n, 2)),
            dma,
            dma((2, 2)),
            dma((2, 2)),
            dma,
        ],
        compiler_params=pltpu.CompilerParams(
            collective_id=0, has_side_effects=True, vmem_limit_bytes=60 * 1024 * 1024
        ),
        cost_estimate=pl.CostEstimate(flops=flops, bytes_accessed=40 << 20, transcendentals=0),
    )(out_grad, gate_pre, up_pre, down_weight)


def solution(mesh):
    return jax.shard_map(
        shards,
        mesh=mesh,
        in_specs=(P(("dp", "mp"), None), P("dp", "mp"), P("dp", "mp"), P("mp", "dp")),
        out_specs=(P("dp", "mp"), P("dp", "mp"), P("mp", "dp")),
        check_vma=False,
    )
```

```python
import itertools
import math

import jax
import jax.numpy as jnp
from jax import lax
from jax.experimental import pallas as pl
from jax.experimental.pallas import tpu as pltpu
from jax.sharding import PartitionSpec as P

MESH = pl.DeviceIdType.MESH
F32 = jnp.float32
BF16 = jnp.bfloat16

ORDER = ((2, 1), (2, 0), (1, 1), (-1, 1), (1, 0), (-1, 0), (0, 1), (0, 0))
SLOT = {at: k for k, at in enumerate(ORDER)}
SPLIT = 832
SCHEDULE = (
    ("O0", 2), ("Wz", 0), ("O0", 0), ("O0", 3), ("Wz", 1), ("H", 0), ("O0", 1), ("H", 1), ("H", 2), ("Wy", 1),
    ("O1b", 0), ("O1a", 2), ("O0", 4), ("Wy", 0), ("O1b", 2), ("O1a", 0), ("H", 3), ("O0", 6), ("O2", 0), ("Wp", 1),
    ("H", 4), ("Wq", -1), ("H", 5), ("Wr", 0), ("O1b", 1), ("O3", 0), ("O1b", 6), ("H", 6), ("Wp", 0), ("O1a", 1),
    ("O2", 1), ("O2", 2), ("T", 0), ("O1b", 3), ("Wq", 1), ("P", 0, 0), ("Ws", 0, 0), ("P", 0, 1), ("Ws", -1, 0),
    ("O1a", 3), ("O3", 1), ("O0", 7), ("O2", 6), ("T", 1), ("O3", 2), ("P", 1, 1), ("O0", 5), ("Wr", 1), ("O2", 3),
    ("O1a", 6), ("T", 2), ("Wq", 2), ("O1b", 4), ("Wc", 1), ("O1a", 4), ("P", 2, 1), ("Wy", 2), ("Wc", -1),
    ("Ws", -1, 1), ("P", 1, 0), ("Ws", 1, 1), ("O3", 3), ("T", 3), ("O1b", 5), ("O2", 4), ("O3", 6), ("Ws", 2, 0),
    ("P", 3, 1), ("P", 2, 0), ("O1a", 5), ("O2", 5), ("O3", 4), ("Ws", 1, 0), ("O1b", 7), ("T", 4), ("O3", 5),
    ("T", 5), ("P", 3, 0), ("O1a", 7), ("Wc", 2), ("O2", 7), ("T", 6), ("P", 5, 1), ("Ws", 2, 1), ("P", 4, 1),
    ("P", 5, 0), ("P", 4, 0), ("P", 6, 1), ("Wc", 0), ("Ws", 0, 1), ("O3", 7), ("T", 7), ("WD",), ("D", 0), ("D", 1),
    ("D", 2), ("P", 6, 0), ("D", 3), ("D", 4), ("P", 7, 1), ("D", 5), ("D", 6), ("P", 7, 0),
)


def kernel(
    og, gp, up, w, gg, gu, gd,
    o_all, w_all, h_t, own, pre, snd, half_in, full_in, y_in, acc, gbuf, ubuf, ggbuf, gubuf,
    o_send, o_recv, w_send, w_recv, wc_send, wc_recv, t_send, t_recv, z_send, z_recv, y_send, y_recv,
    o_local, w_local, in_sem, out_sem, gd_sem,
):
    TB = og.shape[0]
    BLK = w.shape[1]
    FFD = w.shape[0]
    TOK = gp.shape[0]
    HALF = FFD // 2
    TH = TB // 2
    NT = FFD // BLK
    norm = 1.0 / math.sqrt(TOK * 16)

    dp = lax.axis_index("dp")
    mp = lax.axis_index("mp")
    z, yl, c = dp // 4, (dp // 2) % 2, dp % 2
    yh, x = mp // 4, mp % 4

    def dev(dz=0, o=0, cc=0, h=0, dx=0):
        a = ((z + dz + 4) % 4) * 4 + ((yl + o) % 2) * 2 + (c + cc) % 2
        b = ((yh + h) % 2) * 4 + (x + dx + 4) % 4
        return (a, b)

    ZP, ZM, YP, CP = dev(dz=1), dev(dz=-1), dev(o=1), dev(cc=1)
    HP, XP, XM = dev(h=1), dev(dx=1), dev(dx=-1)

    sends = []

    def send(src, dst, ss, rs, to):
        cp = pltpu.make_async_remote_copy(src, dst, ss, rs, device_id=to, device_id_type=MESH)
        cp.start()
        sends.append(cp)
        return cp

    def arrived(dst, ss, rs):
        pltpu.make_async_remote_copy(dst, dst, ss, rs, device_id=CP, device_id_type=MESH).wait_recv()

    barrier = pltpu.get_barrier_semaphore()
    for to in (ZP, ZM, YP, CP, HP, XP, XM):
        pl.semaphore_signal(barrier, inc=1, device_id=to, device_id_type=MESH)

    def tile_in(n, slot):
        cols = pl.ds(pl.multiple_of(n * BLK, BLK), BLK)
        return (
            pltpu.make_async_copy(gp.at[:, cols], gbuf.at[slot], in_sem.at[slot, 0]),
            pltpu.make_async_copy(up.at[:, cols], ubuf.at[slot], in_sem.at[slot, 1]),
        )

    def tile_out(n, slot):
        cols = pl.ds(pl.multiple_of(n * BLK, BLK), BLK)
        return (
            pltpu.make_async_copy(ggbuf.at[slot], gg.at[:, cols], out_sem.at[slot, 0]),
            pltpu.make_async_copy(gubuf.at[slot], gu.at[:, cols], out_sem.at[slot, 1]),
        )

    def o_cols(k):
        return pl.ds(k * 2 * BLK, 2 * BLK)

    def o_rows(h, dx, part=None):
        base = (((yh + h) % 2) * 4 + (x + dx + 4) % 4) * TB
        if part is None:
            return pl.ds(pl.multiple_of(base, TB), TB)
        return pl.ds(pl.multiple_of(base + part * TH, TH), TH)

    def w_cols(k, cc):
        return pl.ds((2 * k + cc) * BLK, BLK)

    w_own = pltpu.make_async_copy(w, w_all.at[:, w_cols(SLOT[0, 0], 0)], w_local)
    w_own.start()
    o_own = []
    for k, (dz, o) in enumerate(ORDER):
        for cc in range(2):
            d = ((z + dz + 4) % 4) * 4 + ((yl + o) % 2) * 2 + (c + cc) % 2
            cp = pltpu.make_async_copy(
                og.at[:, pl.ds(pl.multiple_of(d * BLK, BLK), BLK)],
                o_all.at[o_rows(0, 0), pl.ds((2 * k + cc) * BLK, BLK)],
                o_local.at[k, cc],
            )
            cp.start()
            o_own.append(cp)
    for slot in range(2):
        for cp in tile_in(slot, slot):
            cp.start()

    pl.semaphore_wait(barrier, 7)

    def w_part(dz, o, part):
        if o == 0:
            rows = pl.ds(part * HALF, HALF)
        elif part < 2:
            rows = pl.ds(part * (SPLIT // 2), SPLIT // 2)
        else:
            rows = pl.ds(SPLIT, FFD - SPLIT)
        return w_all.at[rows, w_cols(SLOT[dz, o], 0)]

    n_w = itertools.count()

    def w_to(src, dz, o, part, to):
        send(src, w_part(dz, o, part), w_send.at[next(n_w)], w_recv.at[SLOT[dz, o], part], to)

    w_seen = set()

    def w_got(dz, o, part):
        if (dz, o, part) not in w_seen:
            w_seen.add((dz, o, part))
            arrived(w_part(dz, o, part), w_send.at[0], w_recv.at[SLOT[dz, o], part])

    def Wz(p):
        w_to(w.at[pl.ds(p * HALF, HALF), :], -1, 0, p, ZP)
        w_to(w.at[pl.ds((1 - p) * HALF, HALF), :], 1, 0, 1 - p, ZM)

    def Wy(p):
        rows = (pl.ds(0, SPLIT // 2), pl.ds(SPLIT // 2, SPLIT // 2), pl.ds(SPLIT, FFD - SPLIT))[p]
        w_to(w.at[rows, :], 0, 1, p, YP)

    def Wr(o):
        w_got(-1, o, 0)
        w_to(w_part(-1, o, 0), 2, o, 0, ZP)
        w_got(1, o, 1)
        w_to(w_part(1, o, 1), 2, o, 1, ZM)

    def Wp(p):
        w_got(0, 1, p)
        for dz, to in ((-1, ZP), (1, ZM)) if p == 0 else ((1, ZM), (-1, ZP)):
            w_to(w_part(0, 1, p), dz, 1, p, to)

    def Wq(dz):
        w_got(dz, 0, 0)
        w_got(dz, 0, 1)
        src = w_all.at[pl.ds(SPLIT, FFD - SPLIT), w_cols(SLOT[dz, 0], 0)]
        w_to(src, dz, 1, 2, YP)

    def Wc(dz):
        for p in range(3):
            w_got(dz, 1, p)

    def Ws(dz, o):
        k = SLOT[dz, o]
        if (dz, o) == (0, 0):
            w_own.wait()
        send(w_all.at[:, w_cols(k, 0)], w_all.at[:, w_cols(k, 1)], wc_send.at[k], wc_recv.at[k], CP)

    def WD():
        for k in range(len(ORDER)):
            arrived(w_all.at[:, w_cols(k, 1)], wc_send.at[k], wc_recv.at[k])

    def o_to(k, h, dx, part, kind, to):
        ref = o_all.at[o_rows(h, dx, part), o_cols(k)]
        send(ref, ref, o_send.at[k, kind], o_recv.at[k, kind], to)

    def o_got(k, h, dx, part, kind):
        ref = o_all.at[o_rows(h, dx, part), o_cols(k)]
        arrived(ref, o_send.at[k, kind], o_recv.at[k, kind])

    def O0(k):
        o_own[2 * k].wait()
        o_own[2 * k + 1].wait()
        o_to(k, 0, 0, None, 0, HP)
        o_to(k, 0, 0, None, 1, XP)
        o_to(k, 0, 0, None, 2, XM)

    def O1a(k):
        o_got(k, 0, -1, None, 1)
        o_to(k, 0, -1, 0, 3, XP)
        o_got(k, 0, 1, None, 2)
        o_to(k, 0, 1, 1, 4, XM)

    def O1b(k):
        o_got(k, 1, 0, None, 0)
        o_to(k, 1, 0, None, 5, XP)
        o_to(k, 1, 0, None, 6, XM)

    def O2(k):
        o_got(k, 1, -1, None, 5)
        o_to(k, 1, -1, 0, 7, XP)
        o_got(k, 1, 1, None, 6)
        o_to(k, 1, 1, 1, 8, XM)

    def O3(k):
        o_got(k, 0, 2, 0, 3)
        o_got(k, 0, 2, 1, 4)
        o_got(k, 1, 2, 0, 7)
        o_got(k, 1, 2, 1, 8)

    def H(n):
        slot = n % 2
        for cp in tile_in(n, slot):
            cp.wait()

        def rows(i, _):
            r = pl.ds(pl.multiple_of(i * 128, 128), 128)
            g = gbuf[slot, r, :].astype(F32)
            u = ubuf[slot, r, :].astype(F32)
            hid = g * jax.nn.sigmoid(g) * u
            h_t[pl.ds(pl.multiple_of(n * BLK, BLK), BLK), r] = hid.T.astype(BF16)
            return 0

        lax.fori_loop(0, TOK // 128, rows, 0)

        if n + 2 < NT:
            for cp in tile_in(n + 2, slot):
                cp.start()
        elif n == NT - 1:
            for first in range(2):
                for cp in tile_in(first, first):
                    cp.start()

    def term(k, cc, dst):
        def rows(i, _):
            r = pl.ds(pl.multiple_of(i * HALF, HALF), HALF)
            dst[r, :] = jnp.dot(
                h_t[r, :], o_all[:, pl.ds((2 * k + cc) * BLK, BLK)], preferred_element_type=F32
            ).astype(BF16)
            return 0

        lax.fori_loop(0, 2, rows, 0)

    t_copies = {}

    def T(k):
        slot = k % 2
        if k >= 2:
            t_copies[k - 2].wait_send()
            sends[:] = [cp for cp in sends if cp is not t_copies[k - 2]]
        term(k, 1, snd.at[slot])
        t_copies[k] = send(snd.at[slot], pre.at[k], t_send.at[k], t_recv.at[k], CP)
        term(k, 0, own.at[k])

    def add(dst, parts, scale=None):
        step = 128

        def rows(i, _):
            r = pl.ds(pl.multiple_of(i * step, step), step)
            total = dst[r, :].astype(F32)
            for ref in parts:
                total += ref[r, :].astype(F32)
            if scale is not None:
                total *= scale
            dst[r, :] = total.astype(BF16)
            return 0

        lax.fori_loop(0, HALF // step, rows, 0)

    t_got = set()
    gd_copies = []

    def Pk(k, p):
        dz, o = ORDER[k]
        rows = pl.ds(p * HALF, HALF)
        blk = own.at[k, rows, :]
        if k not in t_got:
            arrived(pre.at[k], t_send.at[k], t_recv.at[k])
            t_got.add(k)
        parts = [pre.at[k, rows, :]]

        def take(ref, sem):
            arrived(ref, z_send.at[o, sem], z_recv.at[o, sem])
            parts.append(ref)

        if dz == 2:
            add(blk, parts)
            send(blk, half_in.at[o, p], z_send.at[o, p], z_recv.at[o, p], (ZP, ZM)[p])
        elif dz:
            side = 0 if dz == 1 else 1
            if p == side:
                take(half_in.at[o, p], p)
            add(blk, parts)
            sem = 2 + 2 * side + p
            dst = full_in.at[o, side, rows, :]
            send(blk, dst, z_send.at[o, sem], z_recv.at[o, sem], (ZP, ZM)[side])
        else:
            for side in range(2):
                take(full_in.at[o, side, rows, :], 2 + 2 * side + p)
            if o == 1:
                add(blk, parts)
                send(blk, y_in.at[rows, :], y_send.at[p], y_recv.at[p], YP)
            else:
                arrived(y_in.at[rows, :], y_send.at[p], y_recv.at[p])
                parts.append(y_in.at[rows, :])
                add(blk, parts, norm)
                cp = pltpu.make_async_copy(blk, gd.at[rows, :], gd_sem.at[p])
                cp.start()
                gd_copies.append(cp)

    def D(n):
        slot = n % 2

        def mm(i, _):
            r = pl.ds(pl.multiple_of(i * 512, 512), 512)
            acc[r, :] = lax.dot_general(
                o_all[r, :],
                w_all[pl.ds(pl.multiple_of(n * BLK, BLK), BLK), :],
                (((1,), (1,)), ((), ())),
                preferred_element_type=F32,
            )
            return 0

        lax.fori_loop(0, TOK // 512, mm, 0)
        for cp in tile_in(n, slot):
            cp.wait()

        if n >= 2:
            for cp in tile_out(n - 2, slot):
                cp.wait()

        def rows(i, _):
            r = pl.ds(pl.multiple_of(i * 64, 64), 64)
            g = gbuf[slot, r, :].astype(F32)
            u = ubuf[slot, r, :].astype(F32)
            d = acc[r, :]
            s = jax.nn.sigmoid(g)
            ggbuf[slot, r, :] = (d * u * s * (1.0 + g * (1.0 - s))).astype(BF16)
            gubuf[slot, r, :] = (d * (g * s)).astype(BF16)
            return 0

        lax.fori_loop(0, TOK // 64, rows, 0)
        for cp in tile_out(n, slot):
            cp.start()
        if n + 2 < NT:
            for cp in tile_in(n + 2, slot):
                cp.start()

    tasks = dict(
        O0=O0, O1a=O1a, O1b=O1b, O2=O2, O3=O3, H=H, T=T, P=Pk, D=D,
        Wz=Wz, Wy=Wy, Wr=Wr, Wp=Wp, Wq=Wq, Wc=Wc, Ws=Ws, WD=WD,
    )
    for name, *at in SCHEDULE:
        tasks[name](*at)
    for cp in tile_out(NT - 2, (NT - 2) % 2) + tile_out(NT - 1, (NT - 1) % 2):
        cp.wait()
    for cp in gd_copies:
        cp.wait()
    for cp in sends:
        cp.wait_send()


def shards(out_grad, gate_pre, up_pre, down_weight):
    TB, D = out_grad.shape
    TOK, FFD = gate_pre.shape
    BLK = down_weight.shape[1]
    n = len(ORDER)
    any_spec = pl.BlockSpec(memory_space=pl.ANY)
    dma = pltpu.SemaphoreType.DMA
    flops = 4 * TOK * D * FFD
    return pl.pallas_call(
        kernel,
        out_shape=(
            jax.ShapeDtypeStruct((TOK, FFD), BF16),
            jax.ShapeDtypeStruct((TOK, FFD), BF16),
            jax.ShapeDtypeStruct((FFD, BLK), BF16),
        ),
        in_specs=[any_spec] * 4,
        out_specs=(any_spec,) * 3,
        scratch_shapes=[
            pltpu.VMEM((TOK, D), BF16),
            pltpu.VMEM((FFD, D), BF16),
            pltpu.VMEM((FFD, TOK), BF16),
            pltpu.VMEM((n, FFD, BLK), BF16),
            pltpu.VMEM((n, FFD, BLK), BF16),
            pltpu.VMEM((2, FFD, BLK), BF16),
            pltpu.VMEM((2, 2, FFD // 2, BLK), BF16),
            pltpu.VMEM((2, 2, FFD, BLK), BF16),
            pltpu.VMEM((FFD, BLK), BF16),
            pltpu.VMEM((TOK, BLK), F32),
            pltpu.VMEM((2, TOK, BLK), BF16),
            pltpu.VMEM((2, TOK, BLK), BF16),
            pltpu.VMEM((2, TOK, BLK), BF16),
            pltpu.VMEM((2, TOK, BLK), BF16),
            dma((n, 9)),
            dma((n, 9)),
            dma((18,)),
            dma((n, 3)),
            dma((n,)),
            dma((n,)),
            dma((n,)),
            dma((n,)),
            dma((2, 6)),
            dma((2, 6)),
            dma((2,)),
            dma((2,)),
            dma((n, 2)),
            dma,
            dma((2, 2)),
            dma((2, 2)),
            dma((2,)),
        ],
        compiler_params=pltpu.CompilerParams(
            collective_id=0, has_side_effects=True, vmem_limit_bytes=60 * 1024 * 1024
        ),
        cost_estimate=pl.CostEstimate(flops=flops, bytes_accessed=40 << 20, transcendentals=0),
    )(out_grad, gate_pre, up_pre, down_weight)


def solution(mesh):
    return jax.shard_map(
        shards,
        mesh=mesh,
        in_specs=(P(("dp", "mp"), None), P("dp", "mp"), P("dp", "mp"), P("mp", "dp")),
        out_specs=(P("dp", "mp"), P("dp", "mp"), P("mp", "dp")),
        check_vma=False,
    )
```

```python
import functools
import itertools
import math

import jax
import jax.numpy as jnp
from jax import lax
from jax.experimental import pallas as pl
from jax.experimental.pallas import tpu as pltpu
from jax.sharding import PartitionSpec as P

MESH = pl.DeviceIdType.MESH
F32 = jnp.float32
BF16 = jnp.bfloat16

ORDER = ((2, 1), (2, 0), (1, 1), (-1, 1), (1, 0), (-1, 0), (0, 1), (0, 0))
SLOT = {at: k for k, at in enumerate(ORDER)}
SPLIT = 1088
SPLIT2 = 1408
VMEM_LIMIT = 51 << 20
SCHEDULE = (
    ("Wz", 0), ("O0", 0), ("O0", 3), ("Ws", 0, 0), ("O0", 2), ("O0", 1), ("H", 0), ("Wy", 0), ("Wy", 1), ("Wz", 1),
    ("Wy", 2), ("H", 1), ("H", 2), ("O1b", 0), ("O1a", 0), ("O1b", 1), ("Wr", 0), ("O2", 0), ("O0", 4), ("O2", 1),
    ("H", 3), ("O0", 5), ("O1b", 2), ("Wp", 0), ("H", 4), ("H", 5), ("H", 6), ("O3", 0), ("Wp", 1), ("O1a", 1),
    ("T", 0), ("O0", 6), ("O1b", 3), ("Wq", 2), ("PY", 0), ("O3", 1), ("O2", 2), ("O1a", 3), ("O1a", 2), ("O2", 3),
    ("O1b", 4), ("P", 0, 1), ("O1b", 5), ("P", 0, 0), ("O1a", 4), ("O0", 7), ("T", 1), ("Wc", 0), ("Wr", 1),
    ("O1a", 5), ("O3", 3), ("O3", 2), ("Wq", -1), ("Ws", 2, 0), ("P", 1, 0), ("Wq", 1), ("T", 2), ("O2", 4),
    ("O1b", 6), ("T", 3), ("P", 1, 1), ("O2", 5), ("P", 3, 0), ("P", 2, 0), ("PY", 3), ("Wc", 2), ("Ws", 0, 1),
    ("PY", 2), ("O3", 4), ("Ws", 2, 1), ("P", 2, 1), ("P", 3, 1), ("Ws", -1, 0), ("O1b", 7), ("T", 4), ("O1a", 6),
    ("O2", 6), ("O3", 5), ("Ws", 1, 0), ("O1a", 7), ("Wc", -1), ("Ws", -1, 1), ("T", 5), ("P", 4, 0), ("O2", 7),
    ("O3", 6), ("T", 6), ("P", 5, 0), ("O3", 7), ("Wc", 1), ("Ws", 1, 1), ("T", 7), ("P", 6, 0), ("WD",), ("D", 0),
    ("PY", 6), ("P", 5, 1), ("D", 1), ("P", 6, 1), ("Z", 0), ("P", 4, 1), ("D", 2), ("D", 3), ("D", 4), ("D", 5),
    ("D", 6), ("Z", 1),
)


def kernel(
    og, gp, up, w, gg, gu, last, up_in, down_in, y_in,
    o_all, w_all, h_t, own, pre, snd, half_in, full_in, y_early, acc, gbuf, ubuf, ggbuf, gubuf,
    o_send, o_recv, w_send, w_recv, wc_send, wc_recv, t_send, t_recv, z_send, z_recv, y_send, y_recv,
    o_local, w_local, in_sem, out_sem, last_sem,
):
    TB = og.shape[0]
    BLK = w.shape[1]
    FFD = w.shape[0]
    TOK = gp.shape[0]
    HALF = FFD // 2
    TH = TB // 2
    NT = FFD // BLK

    dp = lax.axis_index("dp")
    mp = lax.axis_index("mp")
    z, yl, c = dp // 4, (dp // 2) % 2, dp % 2
    yh, x = mp // 4, mp % 4

    def dev(dz=0, o=0, cc=0, h=0, dx=0):
        a = ((z + dz + 4) % 4) * 4 + ((yl + o) % 2) * 2 + (c + cc) % 2
        b = ((yh + h) % 2) * 4 + (x + dx + 4) % 4
        return (a, b)

    ZP, ZM, YP, CP = dev(dz=1), dev(dz=-1), dev(o=1), dev(cc=1)
    HP, XP, XM = dev(h=1), dev(dx=1), dev(dx=-1)

    sends = []

    def send(src, dst, ss, rs, to):
        cp = pltpu.make_async_remote_copy(src, dst, ss, rs, device_id=to, device_id_type=MESH)
        cp.start()
        sends.append(cp)
        return cp

    def arrived(dst, ss, rs):
        pltpu.make_async_remote_copy(dst, dst, ss, rs, device_id=CP, device_id_type=MESH).wait_recv()

    barrier = pltpu.get_barrier_semaphore()
    for to in (ZP, ZM, YP, CP, HP, XP, XM):
        pl.semaphore_signal(barrier, inc=1, device_id=to, device_id_type=MESH)

    def tile_in(n, slot):
        cols = pl.ds(pl.multiple_of(n * BLK, BLK), BLK)
        return (
            pltpu.make_async_copy(gp.at[:, cols], gbuf.at[slot], in_sem.at[slot, 0]),
            pltpu.make_async_copy(up.at[:, cols], ubuf.at[slot], in_sem.at[slot, 1]),
        )

    def tile_out(n, slot):
        cols = pl.ds(pl.multiple_of(n * BLK, BLK), BLK)
        return (
            pltpu.make_async_copy(ggbuf.at[slot], gg.at[:, cols], out_sem.at[slot, 0]),
            pltpu.make_async_copy(gubuf.at[slot], gu.at[:, cols], out_sem.at[slot, 1]),
        )

    def o_cols(k):
        return pl.ds(k * 2 * BLK, 2 * BLK)

    def o_rows(h, dx, part=None):
        base = (((yh + h) % 2) * 4 + (x + dx + 4) % 4) * TB
        if part is None:
            return pl.ds(pl.multiple_of(base, TB), TB)
        return pl.ds(pl.multiple_of(base + part * TH, TH), TH)

    def w_cols(k, cc):
        return pl.ds((2 * k + cc) * BLK, BLK)

    w_own = pltpu.make_async_copy(w, w_all.at[:, w_cols(SLOT[0, 0], 0)], w_local)
    w_own.start()
    o_own = []
    for k, (dz, o) in enumerate(ORDER):
        for cc in range(2):
            d = ((z + dz + 4) % 4) * 4 + ((yl + o) % 2) * 2 + (c + cc) % 2
            cp = pltpu.make_async_copy(
                og.at[:, pl.ds(pl.multiple_of(d * BLK, BLK), BLK)],
                o_all.at[o_rows(0, 0), pl.ds((2 * k + cc) * BLK, BLK)],
                o_local.at[k, cc],
            )
            cp.start()
            o_own.append(cp)
    for slot in range(2):
        for cp in tile_in(slot, slot):
            cp.start()

    pl.semaphore_wait(barrier, 7)

    def w_part(dz, o, part):
        if o == 0:
            rows = pl.ds(part * HALF, HALF)
        elif part < 2:
            rows = pl.ds(part * (SPLIT // 2), SPLIT // 2)
        else:
            rows = pl.ds(SPLIT, FFD - SPLIT)
        return w_all.at[rows, w_cols(SLOT[dz, o], 0)]

    n_w = itertools.count()

    def w_to(src, dz, o, part, to):
        send(src, w_part(dz, o, part), w_send.at[next(n_w)], w_recv.at[SLOT[dz, o], part], to)

    w_seen = set()

    def w_got(dz, o, part):
        if (dz, o, part) not in w_seen:
            w_seen.add((dz, o, part))
            arrived(w_part(dz, o, part), w_send.at[0], w_recv.at[SLOT[dz, o], part])

    def Wz(p):
        w_to(w.at[pl.ds(p * HALF, HALF), :], -1, 0, p, ZP)
        w_to(w.at[pl.ds((1 - p) * HALF, HALF), :], 1, 0, 1 - p, ZM)

    def Wy(p):
        rows = (pl.ds(0, SPLIT // 2), pl.ds(SPLIT // 2, SPLIT // 2), pl.ds(SPLIT, FFD - SPLIT))[p]
        w_to(w.at[rows, :], 0, 1, p, YP)

    def Wr(o):
        w_got(-1, o, 0)
        w_to(w_part(-1, o, 0), 2, o, 0, ZP)
        w_got(1, o, 1)
        w_to(w_part(1, o, 1), 2, o, 1, ZM)

    def Wp(p):
        w_got(0, 1, p)
        for dz, to in ((-1, ZP), (1, ZM)) if p == 0 else ((1, ZM), (-1, ZP)):
            w_to(w_part(0, 1, p), dz, 1, p, to)

    def Wq(dz):
        w_got(dz, 0, 0)
        w_got(dz, 0, 1)
        src = w_all.at[pl.ds(SPLIT, FFD - SPLIT), w_cols(SLOT[dz, 0], 0)]
        w_to(src, dz, 1, 2, YP)

    def Wc(dz):
        for p in range(3):
            w_got(dz, 1, p)

    def Ws(dz, o):
        k = SLOT[dz, o]
        if (dz, o) == (0, 0):
            w_own.wait()
        send(w_all.at[:, w_cols(k, 0)], w_all.at[:, w_cols(k, 1)], wc_send.at[k], wc_recv.at[k], CP)

    def WD():
        for k in range(len(ORDER)):
            arrived(w_all.at[:, w_cols(k, 1)], wc_send.at[k], wc_recv.at[k])

    def o_to(k, h, dx, part, kind, to):
        ref = o_all.at[o_rows(h, dx, part), o_cols(k)]
        send(ref, ref, o_send.at[k, kind], o_recv.at[k, kind], to)

    def o_got(k, h, dx, part, kind):
        ref = o_all.at[o_rows(h, dx, part), o_cols(k)]
        arrived(ref, o_send.at[k, kind], o_recv.at[k, kind])

    def O0(k):
        o_own[2 * k].wait()
        o_own[2 * k + 1].wait()
        o_to(k, 0, 0, None, 0, HP)
        o_to(k, 0, 0, None, 1, XP)
        o_to(k, 0, 0, None, 2, XM)

    def O1a(k):
        o_got(k, 0, -1, None, 1)
        o_to(k, 0, -1, 0, 3, XP)
        o_got(k, 0, 1, None, 2)
        o_to(k, 0, 1, 1, 4, XM)

    def O1b(k):
        o_got(k, 1, 0, None, 0)
        o_to(k, 1, 0, None, 5, XP)
        o_to(k, 1, 0, None, 6, XM)

    def O2(k):
        o_got(k, 1, -1, None, 5)
        o_to(k, 1, -1, 0, 7, XP)
        o_got(k, 1, 1, None, 6)
        o_to(k, 1, 1, 1, 8, XM)

    def O3(k):
        o_got(k, 0, 2, 0, 3)
        o_got(k, 0, 2, 1, 4)
        o_got(k, 1, 2, 0, 7)
        o_got(k, 1, 2, 1, 8)

    def H(n):
        slot = n % 2
        for cp in tile_in(n, slot):
            cp.wait()

        def rows(i, _):
            r = pl.ds(pl.multiple_of(i * 128, 128), 128)
            g = gbuf[slot, r, :].astype(F32)
            u = ubuf[slot, r, :].astype(F32)
            hid = g * jax.nn.sigmoid(g) * u
            h_t[pl.ds(pl.multiple_of(n * BLK, BLK), BLK), r] = hid.T.astype(BF16)
            return 0

        lax.fori_loop(0, TOK // 128, rows, 0)

        if n + 2 < NT:
            for cp in tile_in(n + 2, slot):
                cp.start()
        elif n == NT - 1:
            for first in range(2):
                for cp in tile_in(first, first):
                    cp.start()

    def term(k, cc, dst):
        def rows(i, _):
            r = pl.ds(pl.multiple_of(i * HALF, HALF), HALF)
            dst[r, :] = jnp.dot(
                h_t[r, :], o_all[:, pl.ds((2 * k + cc) * BLK, BLK)], preferred_element_type=F32
            ).astype(BF16)
            return 0

        lax.fori_loop(0, 2, rows, 0)

    t_copies = {}

    def T(k):
        slot = k % 2
        if k >= 2:
            t_copies[k - 2].wait_send()
            sends[:] = [cp for cp in sends if cp is not t_copies[k - 2]]
        term(k, 1, snd.at[slot])
        t_copies[k] = send(snd.at[slot], pre.at[k], t_send.at[k], t_recv.at[k], CP)
        term(k, 0, own.at[k])

    def row_part(o, p):
        if o == 0:
            return p * HALF, HALF
        return (p * (SPLIT2 // 2), SPLIT2 // 2) if p < 2 else (SPLIT2, FFD - SPLIT2)

    def add(k, at, size, others):
        step = 64
        others = [(pre.at[k], 0, FFD), *others]
        cuts = {at, at + size}
        for _, first, many in others:
            cuts |= {row for row in (first, first + many) if at < row < at + size}
        cuts = sorted(cuts)
        for low, high in zip(cuts, cuts[1:]):
            inside = [(ref, first) for ref, first, many in others if first <= low and high <= first + many]

            def rows(i, _, low=low, inside=inside):
                r = pl.ds(pl.multiple_of(low + i * step, step), step)
                total = own[k, r, :].astype(F32)
                for ref, first in inside:
                    total += ref[pl.ds(pl.multiple_of(low - first + i * step, step), step), :].astype(F32)
                own[k, r, :] = total.astype(BF16)
                return 0

            lax.fori_loop(0, (high - low) // step, rows, 0)

    seen = set()
    last_copies = []

    def once(ref, ss, rs, *name):
        if name not in seen:
            seen.add(name)
            arrived(ref, ss, rs)

    def y_part(dz, p):
        if dz == 0:
            at, size = row_part(1, p)
            return y_in.at[pl.ds(at, size), :], p
        i = (2, 1, -1).index(dz)
        return y_early.at[i], 3 + i

    def y_got(dz, p):
        ref, sem = y_part(dz, p)
        once(ref, y_send.at[sem], y_recv.at[sem], "y", sem)

    def y_to(k, dz, p):
        at, size = row_part(1, p)
        ref, sem = y_part(dz, p)
        send(own.at[k, pl.ds(at, size), :], ref, y_send.at[sem], y_recv.at[sem], YP)

    def PY(k):
        once(pre.at[k], t_send.at[k], t_recv.at[k], "t", k)
        at, size = row_part(1, 2)
        add(k, at, size, [])
        y_to(k, ORDER[k][0], 2)

    def Pk(k, p):
        dz, o = ORDER[k]
        at, size = row_part(o, p)
        rows = pl.ds(at, size)
        blk = own.at[k, rows, :]
        once(pre.at[k], t_send.at[k], t_recv.at[k], "t", k)
        others = []
        if o == 0 and dz and p == 1:
            y_got(dz, 2)
            others.append((y_part(dz, 2)[0], SPLIT2, FFD - SPLIT2))
        if dz == 2:
            add(k, at, size, others)
            send(blk, half_in.at[o, p, pl.ds(0, size), :], z_send.at[o, p], z_recv.at[o, p], (ZP, ZM)[p])
        elif dz:
            side = 0 if dz == 1 else 1
            if p == side:
                ref = half_in.at[o, p, pl.ds(0, size), :]
                arrived(ref, z_send.at[o, p], z_recv.at[o, p])
                others.append((ref, at, size))
            add(k, at, size, others)
            sem = 2 + 2 * side + p
            dst = full_in.at[side, rows, :] if o else (up_in, down_in)[side].at[rows, :]
            send(blk, dst, z_send.at[o, sem], z_recv.at[o, sem], (ZP, ZM)[side])
        else:
            for side in range(2):
                sem = 2 + 2 * side + p
                arrived(full_in.at[side, rows, :], z_send.at[o, sem], z_recv.at[o, sem])
                others.append((full_in.at[side], 0, FFD))
            add(k, at, size, others)
            y_to(k, 0, p)

    def Z(p):
        k = SLOT[0, 0]
        if p == 0:
            once(pre.at[k], t_send.at[k], t_recv.at[k], "t", k)
            add(k, 0, FFD, [])
            cp = pltpu.make_async_copy(own.at[k], last, last_sem)
            cp.start()
            last_copies.append(cp)
            return
        for half in range(2):
            rows = pl.ds(half * HALF, HALF)
            for side, ref in enumerate((up_in, down_in)):
                sem = 2 + 2 * side + half
                arrived(ref.at[rows, :], z_send.at[0, sem], z_recv.at[0, sem])
        for part in range(3):
            y_got(0, part)

    def D(n):
        slot = n % 2

        def mm(i, _):
            r = pl.ds(pl.multiple_of(i * 512, 512), 512)
            acc[r, :] = lax.dot_general(
                o_all[r, :],
                w_all[pl.ds(pl.multiple_of(n * BLK, BLK), BLK), :],
                (((1,), (1,)), ((), ())),
                preferred_element_type=F32,
            )
            return 0

        lax.fori_loop(0, TOK // 512, mm, 0)
        for cp in tile_in(n, slot):
            cp.wait()

        if n >= 2:
            for cp in tile_out(n - 2, slot):
                cp.wait()

        def rows(i, _):
            r = pl.ds(pl.multiple_of(i * 64, 64), 64)
            g = gbuf[slot, r, :].astype(F32)
            u = ubuf[slot, r, :].astype(F32)
            d = acc[r, :]
            s = jax.nn.sigmoid(g)
            ggbuf[slot, r, :] = (d * u * s * (1.0 + g * (1.0 - s))).astype(BF16)
            gubuf[slot, r, :] = (d * (g * s)).astype(BF16)
            return 0

        lax.fori_loop(0, TOK // 64, rows, 0)
        for cp in tile_out(n, slot):
            cp.start()
        if n + 2 < NT:
            for cp in tile_in(n + 2, slot):
                cp.start()

    tasks = dict(
        O0=O0, O1a=O1a, O1b=O1b, O2=O2, O3=O3, H=H, T=T, P=Pk, PY=PY, Z=Z, D=D,
        Wz=Wz, Wy=Wy, Wr=Wr, Wp=Wp, Wq=Wq, Wc=Wc, Ws=Ws, WD=WD,
    )
    for name, *at in SCHEDULE:
        tasks[name](*at)
    for cp in tile_out(NT - 2, (NT - 2) % 2) + tile_out(NT - 1, (NT - 1) % 2):
        cp.wait()
    for cp in last_copies:
        cp.wait()
    for cp in sends:
        cp.wait_send()


def finish(norm, gg_in, gu_in, last, up_in, down_in, y_in, gg, gu, gd, total, sem):
    copies = [pltpu.make_async_copy(src, dst, sem.at[i]) for i, (src, dst) in enumerate(((gg_in, gg), (gu_in, gu)))]
    for cp in copies:
        cp.start()

    def rows(i, _):
        r = pl.ds(pl.multiple_of(i * 128, 128), 128)
        acc = last[r, :].astype(F32)
        for ref in (up_in, down_in, y_in):
            acc += ref[r, :].astype(F32)
        total[r, :] = (acc * norm).astype(BF16)
        return 0

    lax.fori_loop(0, total.shape[0] // 128, rows, 0)
    copies.append(pltpu.make_async_copy(total, gd, sem.at[2]))
    copies[-1].start()
    for cp in copies:
        cp.wait()


def shards(out_grad, gate_pre, up_pre, down_weight):
    TB, D = out_grad.shape
    TOK, FFD = gate_pre.shape
    BLK = down_weight.shape[1]
    n = len(ORDER)
    any_spec = pl.BlockSpec(memory_space=pl.ANY)
    dma = pltpu.SemaphoreType.DMA
    flops = 4 * TOK * D * FFD
    results = pl.pallas_call(
        kernel,
        out_shape=[pltpu.VMEM((TOK, FFD), BF16)] * 2 + [pltpu.VMEM((FFD, BLK), BF16)] * 4,
        in_specs=[any_spec] * 4,
        out_specs=[any_spec] * 6,
        scratch_shapes=[
            pltpu.VMEM((TOK, D), BF16),
            pltpu.VMEM((FFD, D), BF16),
            pltpu.VMEM((FFD, TOK), BF16),
            pltpu.VMEM((n, FFD, BLK), BF16),
            pltpu.VMEM((n, FFD, BLK), BF16),
            pltpu.VMEM((2, FFD, BLK), BF16),
            pltpu.VMEM((2, 2, FFD // 2, BLK), BF16),
            pltpu.VMEM((2, FFD, BLK), BF16),
            pltpu.VMEM((3, FFD - SPLIT2, BLK), BF16),
            pltpu.VMEM((TOK, BLK), F32),
            pltpu.VMEM((2, TOK, BLK), BF16),
            pltpu.VMEM((2, TOK, BLK), BF16),
            pltpu.VMEM((2, TOK, BLK), BF16),
            pltpu.VMEM((2, TOK, BLK), BF16),
            dma((n, 9)),
            dma((n, 9)),
            dma((18,)),
            dma((n, 3)),
            dma((n,)),
            dma((n,)),
            dma((n,)),
            dma((n,)),
            dma((2, 6)),
            dma((2, 6)),
            dma((6,)),
            dma((6,)),
            dma((n, 2)),
            dma,
            dma((2, 2)),
            dma((2, 2)),
            dma,
        ],
        compiler_params=pltpu.CompilerParams(
            collective_id=0, has_side_effects=True, vmem_limit_bytes=VMEM_LIMIT
        ),
        cost_estimate=pl.CostEstimate(flops=flops, bytes_accessed=40 << 20, transcendentals=0),
    )(out_grad, gate_pre, up_pre, down_weight)
    return pl.pallas_call(
        functools.partial(finish, 1.0 / math.sqrt(TOK * lax.axis_size("dp"))),
        out_shape=[jax.ShapeDtypeStruct(shape, BF16) for shape in ((TOK, FFD), (TOK, FFD), (FFD, BLK))],
        in_specs=[any_spec] * 2 + [pl.BlockSpec(memory_space=pltpu.VMEM)] * 4,
        out_specs=[any_spec] * 3,
        scratch_shapes=[pltpu.VMEM((FFD, BLK), BF16), dma((3,))],
        compiler_params=pltpu.CompilerParams(vmem_limit_bytes=2 << 20),
    )(*(pltpu.with_memory_space_constraint(a, pltpu.VMEM) for a in results))


def solution(mesh):
    return jax.shard_map(
        shards,
        mesh=mesh,
        in_specs=(P(("dp", "mp"), None), P("dp", "mp"), P("dp", "mp"), P("mp", "dp")),
        out_specs=(P("dp", "mp"), P("dp", "mp"), P("mp", "dp")),
        check_vma=False,
    )
```

```python
import functools
import math

import jax
import jax.numpy as jnp
from jax import lax
from jax.experimental import pallas as pl
from jax.experimental.pallas import tpu as pltpu
from jax.sharding import PartitionSpec as P

MESH = pl.DeviceIdType.MESH
F32 = jnp.float32
BF16 = jnp.bfloat16

ORDER = ((2, 1), (2, 0), (1, 1), (-1, 1), (1, 0), (-1, 0), (0, 1), (0, 0))
SLOT = {at: k for k, at in enumerate(ORDER)}
W_GROUPS = (
    ((-1, 0, 0), (1, 0, 1)), ((-1, 0, 1),), ((1, 0, 0),), ((2, 0, 0), (2, 0, 1)), ((0, 1, 0),), ((0, 1, 1),), ((0, 1, 2),),
    ((-1, 1, 0), (1, 1, 1)), ((-1, 1, 1), (-1, 1, 2)), ((1, 1, 0), (1, 1, 2)), ((2, 1, 0), (2, 1, 1), (2, 1, 2)),
)
SPLIT = 1184
SPLIT2 = 1280
FIRST = 1
VMEM_LIMIT = 51 << 20
SCHEDULE = (
    ("Wz", 0), ("O0", 1), ("O0", 3), ("O0", 0), ("H", 0), ("H", 1), ("Wz", 1), ("O0", 2), ("O1b", 3), ("Wy", 0),
    ("Wy", 1), ("O1b", 0), ("O1b", 1), ("O1a", 3), ("H", 2), ("O1a", 0), ("Wr", 0), ("O2", 0), ("Wy", 2), ("O2", 1),
    ("O1a", 2), ("H", 3), ("O2", 3), ("H", 4), ("H", 5), ("O1a", 1), ("O3", 0), ("Wp", 0), ("O1b", 2), ("Wp", 1),
    ("O0", 5), ("O0", 4), ("H", 6), ("T", 0), ("P", 0, 1), ("O3", 1), ("O0", 6), ("PY", 0), ("Wc", 0), ("O0", 7),
    ("Ws", 0, 1), ("T", 1), ("O2", 2), ("P", 0, 0), ("O1b", 5), ("Wq", 2), ("Ws", 0, 0), ("O3", 3), ("Wr", 1),
    ("O1b", 4), ("T", 3), ("P", 1, 0), ("Wq", -1), ("O1a", 5), ("O3", 2), ("P", 1, 1), ("O1b", 6), ("T", 2),
    ("Ws", 2, 0), ("O2", 5), ("Wq", 1), ("O2", 4), ("O1a", 4), ("Ws", -1, 0), ("P", 2, 1), ("O1b", 7), ("P", 3, 1),
    ("O1a", 6), ("Ws", 1, 0), ("PY", 3), ("Wc", 2), ("PY", 2), ("P", 3, 0), ("O3", 5), ("O2", 6), ("Ws", 2, 1),
    ("O1a", 7), ("T", 5), ("O3", 4), ("T", 4), ("P", 2, 0), ("Wc", -1), ("O2", 7), ("P", 5, 0), ("O3", 6),
    ("Ws", -1, 1), ("T", 6), ("Wc", 1), ("O3", 7), ("Ws", 1, 1), ("T", 7), ("P", 4, 0), ("PY", 6), ("WD",), ("D", 0),
    ("D", 1), ("P", 6, 1), ("P", 4, 1), ("D", 2), ("P", 5, 1), ("P", 6, 0), ("Z", 0), ("D", 3), ("D", 4), ("D", 5),
    ("D", 6), ("Z", 1),
)


def kernel(
    og, gp, up, w, gg, gu, last, up_in, down_in, y_in,
    o_all, w_all, h_t, own, pre, snd, half_in, full_in, y_early, acc, gbuf, ubuf, ggbuf, gubuf,
    o_send, w_send, t_send, r_send, o_recv, w_recv, wc_recv, t_recv, half_recv, full_recv, y_recv, end_recv,
    o_local, w_local, in_sem, out_sem, last_sem,
):
    TB = og.shape[0]
    BLK = w.shape[1]
    FFD = w.shape[0]
    TOK = gp.shape[0]
    HALF = FFD // 2
    TH = TB // 2
    NT = FFD // BLK

    dp = lax.axis_index("dp")
    mp = lax.axis_index("mp")
    z, yl, c = dp // 4, (dp // 2) % 2, dp % 2
    yh, x = mp // 4, mp % 4

    def dev(dz=0, o=0, cc=0, h=0, dx=0):
        a = ((z + dz + 4) % 4) * 4 + ((yl + o) % 2) * 2 + (c + cc) % 2
        b = ((yh + h) % 2) * 4 + (x + dx + 4) % 4
        return (a, b)

    ZP, ZM, YP, CP = dev(dz=1), dev(dz=-1), dev(o=1), dev(cc=1)
    HP, XP, XM = dev(h=1), dev(dx=1), dev(dx=-1)

    def send(src, dst, ss, rs, to):
        cp = pltpu.make_async_remote_copy(src, dst, ss, rs, device_id=to, device_id_type=MESH)
        cp.start()
        return cp

    def arrived(like, rs):
        pltpu.make_async_remote_copy(like, like, o_send, rs, device_id=CP, device_id_type=MESH).wait_recv()

    def sent(like, ss):
        pltpu.make_async_remote_copy(like, like, ss, end_recv, device_id=CP, device_id_type=MESH).wait_send()

    barrier = pltpu.get_barrier_semaphore()
    for to in (ZP, ZM, YP, CP, HP, XP, XM):
        pl.semaphore_signal(barrier, inc=1, device_id=to, device_id_type=MESH)

    def tile_in(n, slot):
        cols = pl.ds(pl.multiple_of(n * BLK, BLK), BLK)
        return (
            pltpu.make_async_copy(gp.at[:, cols], gbuf.at[slot], in_sem.at[slot, 0]),
            pltpu.make_async_copy(up.at[:, cols], ubuf.at[slot], in_sem.at[slot, 1]),
        )

    def tile_out(n, slot):
        cols = pl.ds(pl.multiple_of(n * BLK, BLK), BLK)
        return (
            pltpu.make_async_copy(ggbuf.at[slot], gg.at[:, cols], out_sem.at[slot, 0]),
            pltpu.make_async_copy(gubuf.at[slot], gu.at[:, cols], out_sem.at[slot, 1]),
        )

    def o_cols(k):
        return pl.ds(k * 2 * BLK, 2 * BLK)

    def o_rows(h, dx, part=None):
        base = (((yh + h) % 2) * 4 + (x + dx + 4) % 4) * TB
        if part is None:
            return pl.ds(pl.multiple_of(base, TB), TB)
        return pl.ds(pl.multiple_of(base + part * TH, TH), TH)

    def w_cols(k, cc):
        return pl.ds((2 * k + cc) * BLK, BLK)

    w_own = pltpu.make_async_copy(w, w_all.at[:, w_cols(SLOT[0, 0], 0)], w_local)
    w_own.start()
    for k, (dz, o) in enumerate(ORDER):
        for cc in range(2):
            d = ((z + dz + 4) % 4) * 4 + ((yl + o) % 2) * 2 + (c + cc) % 2
            cp = pltpu.make_async_copy(
                og.at[:, pl.ds(pl.multiple_of(d * BLK, BLK), BLK)],
                o_all.at[o_rows(0, 0), pl.ds((2 * k + cc) * BLK, BLK)],
                o_local.at[0 if k == FIRST else 1],
            )
            cp.start()
    for slot in range(2):
        for cp in tile_in(slot, slot):
            cp.start()

    pl.semaphore_wait(barrier, 7)

    def w_part(dz, o, part):
        if o == 0:
            rows = pl.ds(part * HALF, HALF)
        elif part < 2:
            rows = pl.ds(part * (SPLIT // 2), SPLIT // 2)
        else:
            rows = pl.ds(SPLIT, FFD - SPLIT)
        return w_all.at[rows, w_cols(SLOT[dz, o], 0)]

    def w_size(o, part):
        return HALF if o == 0 else SPLIT // 2 if part < 2 else FFD - SPLIT

    w_group = {part: i for i, group in enumerate(W_GROUPS) for part in group}
    w_seen = set()

    def w_to(src, dz, o, part, to):
        send(src, w_part(dz, o, part), w_send, w_recv.at[w_group[dz, o, part]], to)

    def w_got(dz, o, part):
        i = w_group[dz, o, part]
        if i not in w_seen:
            w_seen.add(i)
            rows = sum(w_size(o, part) for _, o, part in W_GROUPS[i])
            arrived(w_all.at[pl.ds(0, rows), pl.ds(0, BLK)], w_recv.at[i])

    def Wz(p):
        w_to(w.at[pl.ds(p * HALF, HALF), :], -1, 0, p, ZP)
        w_to(w.at[pl.ds((1 - p) * HALF, HALF), :], 1, 0, 1 - p, ZM)

    def Wy(p):
        rows = (pl.ds(0, SPLIT // 2), pl.ds(SPLIT // 2, SPLIT // 2), pl.ds(SPLIT, FFD - SPLIT))[p]
        w_to(w.at[rows, :], 0, 1, p, YP)

    def Wr(o):
        w_got(-1, o, 0)
        w_to(w_part(-1, o, 0), 2, o, 0, ZP)
        w_got(1, o, 1)
        w_to(w_part(1, o, 1), 2, o, 1, ZM)

    def Wp(p):
        w_got(0, 1, p)
        for dz, to in ((-1, ZP), (1, ZM)) if p == 0 else ((1, ZM), (-1, ZP)):
            w_to(w_part(0, 1, p), dz, 1, p, to)

    def Wq(dz):
        w_got(dz, 0, 0)
        w_got(dz, 0, 1)
        src = w_all.at[pl.ds(SPLIT, FFD - SPLIT), w_cols(SLOT[dz, 0], 0)]
        w_to(src, dz, 1, 2, YP)

    def Wc(dz):
        for p in range(3):
            w_got(dz, 1, p)

    def Ws(dz, o):
        k = SLOT[dz, o]
        if (dz, o) == (0, 0):
            w_own.wait()
        send(w_all.at[:, w_cols(k, 0)], w_all.at[:, w_cols(k, 1)], w_send, wc_recv, CP)

    def WD():
        arrived(w_all.at[:, pl.ds(0, len(ORDER) * BLK)], wc_recv)

    def o_to(k, h, dx, part, kind, to):
        ref = o_all.at[o_rows(h, dx, part), o_cols(k)]
        send(ref, ref, o_send, o_recv.at[k, kind], to)

    def o_got(k, rows, kind):
        arrived(o_all.at[pl.ds(0, rows), o_cols(k)], o_recv.at[k, kind])

    o_ready = set()

    def O0(k):
        i = 0 if k == FIRST else 1
        if i not in o_ready:
            o_ready.add(i)
            mine = o_all.at[o_rows(0, 0), pl.ds(0, (2 if i == 0 else 14) * BLK)]
            pltpu.make_async_copy(mine, mine, o_local.at[i]).wait()
        o_to(k, 0, 0, None, 0, HP)
        o_to(k, 0, 0, None, 1, XP)
        o_to(k, 0, 0, None, 1, XM)

    def O1a(k):
        o_got(k, 2 * TB, 1)
        o_to(k, 0, -1, 0, 3, XP)
        o_to(k, 0, 1, 1, 3, XM)

    def O1b(k):
        o_got(k, TB, 0)
        o_to(k, 1, 0, None, 2, XP)
        o_to(k, 1, 0, None, 2, XM)

    def O2(k):
        o_got(k, 2 * TB, 2)
        o_to(k, 1, -1, 0, 3, XP)
        o_to(k, 1, 1, 1, 3, XM)

    def O3(k):
        o_got(k, 2 * TB, 3)

    def H(n):
        slot = n % 2
        for cp in tile_in(n, slot):
            cp.wait()

        def rows(i, _):
            r = pl.ds(pl.multiple_of(i * 128, 128), 128)
            g = gbuf[slot, r, :].astype(F32)
            u = ubuf[slot, r, :].astype(F32)
            hid = g * jax.nn.sigmoid(g) * u
            h_t[pl.ds(pl.multiple_of(n * BLK, BLK), BLK), r] = hid.T.astype(BF16)
            return 0

        lax.fori_loop(0, TOK // 128, rows, 0)

        if n + 2 < NT:
            for cp in tile_in(n + 2, slot):
                cp.start()
        elif n == NT - 1:
            for first in range(2):
                for cp in tile_in(first, first):
                    cp.start()

    def term(k, cc, dst):
        def rows(i, _):
            r = pl.ds(pl.multiple_of(i * HALF, HALF), HALF)
            dst[r, :] = jnp.dot(
                h_t[r, :], o_all[:, pl.ds((2 * k + cc) * BLK, BLK)], preferred_element_type=F32
            ).astype(BF16)
            return 0

        lax.fori_loop(0, 2, rows, 0)

    t_copies = {}

    def T(k):
        slot = k % 2
        if k >= 2:
            t_copies.pop(k - 2).wait_send()
        term(k, 1, snd.at[slot])
        t_copies[k] = send(snd.at[slot], pre.at[k], t_send.at[slot], t_recv.at[k], CP)
        term(k, 0, own.at[k])

    def row_part(o, p):
        if o == 0:
            return p * HALF, HALF
        return (p * (SPLIT2 // 2), SPLIT2 // 2) if p < 2 else (SPLIT2, FFD - SPLIT2)

    def add(k, at, size, others):
        step = 32
        others = [(pre.at[k], 0, FFD), *others]
        cuts = {at, at + size}
        for _, first, many in others:
            cuts |= {row for row in (first, first + many) if at < row < at + size}
        cuts = sorted(cuts)
        for low, high in zip(cuts, cuts[1:]):
            inside = [(ref, first) for ref, first, many in others if first <= low and high <= first + many]

            def rows(i, _, low=low, inside=inside):
                r = pl.ds(pl.multiple_of(low + i * step, step), step)
                total = own[k, r, :].astype(F32)
                for ref, first in inside:
                    total += ref[pl.ds(pl.multiple_of(low - first + i * step, step), step), :].astype(F32)
                own[k, r, :] = total.astype(BF16)
                return 0

            lax.fori_loop(0, (high - low) // step, rows, 0)

    seen = set()
    last_copies = []

    def t_got(k):
        if k not in seen:
            seen.add(k)
            arrived(pre.at[k], t_recv.at[k])

    def like(rows):
        return pre.at[0, pl.ds(0, rows), :]

    def y_to(k, dz, p):
        at, size = row_part(1, p)
        src = own.at[k, pl.ds(at, size), :]
        if dz == 0:
            send(src, y_in.at[pl.ds(at, size), :], r_send, end_recv, YP)
        else:
            i = (2, 1, -1).index(dz)
            send(src, y_early.at[i], r_send, y_recv.at[i], YP)

    def PY(k):
        t_got(k)
        at, size = row_part(1, 2)
        add(k, at, size, [])
        y_to(k, ORDER[k][0], 2)

    def Pk(k, p):
        dz, o = ORDER[k]
        at, size = row_part(o, p)
        rows = pl.ds(at, size)
        blk = own.at[k, rows, :]
        t_got(k)
        others = []
        if o == 0 and p == 1:
            i = (2, 1, -1).index(dz)
            arrived(y_early.at[i], y_recv.at[i])
            others.append((y_early.at[i], SPLIT2, FFD - SPLIT2))
        if dz == 2:
            add(k, at, size, others)
            send(blk, half_in.at[o, p, pl.ds(0, size), :], r_send, half_recv.at[o, p], (ZP, ZM)[p])
        elif dz:
            side = 0 if dz == 1 else 1
            if p == side:
                ref = half_in.at[o, p, pl.ds(0, size), :]
                arrived(ref, half_recv.at[o, p])
                others.append((ref, at, size))
            add(k, at, size, others)
            if o == 1:
                send(blk, full_in.at[side, rows, :], r_send, full_recv.at[p], (ZP, ZM)[side])
            else:
                send(blk, (up_in, down_in)[side].at[rows, :], r_send, end_recv, (ZP, ZM)[side])
        else:
            arrived(like(2 * size), full_recv.at[p])
            add(k, at, size, [(full_in.at[side], 0, FFD) for side in range(2)])
            y_to(k, 0, p)

    def Z(p):
        k = SLOT[0, 0]
        if p == 0:
            t_got(k)
            add(k, 0, FFD, [])
            cp = pltpu.make_async_copy(own.at[k], last, last_sem)
            cp.start()
            last_copies.append(cp)
            return
        for cp in tile_out(NT - 2, (NT - 2) % 2) + tile_out(NT - 1, (NT - 1) % 2) + tuple(last_copies):
            cp.wait()
        blocks = len(ORDER)
        sent(o_all.at[pl.ds(0, 7 * TB), :], o_send)
        sent(w_all.at[:, pl.ds(0, (2 * blocks - 1) * BLK)], w_send)
        for cp in t_copies.values():
            cp.wait_send()
        sent(pre.at[pl.ds(0, blocks - 1)], r_send)
        arrived(pre.at[pl.ds(0, 3)], end_recv)

    def D(n):
        slot = n % 2

        def mm(i, _):
            r = pl.ds(pl.multiple_of(i * 512, 512), 512)
            acc[r, :] = lax.dot_general(
                o_all[r, :],
                w_all[pl.ds(pl.multiple_of(n * BLK, BLK), BLK), :],
                (((1,), (1,)), ((), ())),
                preferred_element_type=F32,
            )
            return 0

        lax.fori_loop(0, TOK // 512, mm, 0)
        for cp in tile_in(n, slot):
            cp.wait()

        if n >= 2:
            for cp in tile_out(n - 2, slot):
                cp.wait()

        def rows(i, _):
            r = pl.ds(pl.multiple_of(i * 64, 64), 64)
            g = gbuf[slot, r, :].astype(F32)
            u = ubuf[slot, r, :].astype(F32)
            d = acc[r, :]
            s = jax.nn.sigmoid(g)
            ggbuf[slot, r, :] = (d * u * s * (1.0 + g * (1.0 - s))).astype(BF16)
            gubuf[slot, r, :] = (d * (g * s)).astype(BF16)
            return 0

        lax.fori_loop(0, TOK // 64, rows, 0)
        for cp in tile_out(n, slot):
            cp.start()
        if n + 2 < NT:
            for cp in tile_in(n + 2, slot):
                cp.start()

    tasks = dict(
        O0=O0, O1a=O1a, O1b=O1b, O2=O2, O3=O3, H=H, T=T, P=Pk, PY=PY, Z=Z, D=D,
        Wz=Wz, Wy=Wy, Wr=Wr, Wp=Wp, Wq=Wq, Wc=Wc, Ws=Ws, WD=WD,
    )
    for name, *at in SCHEDULE:
        tasks[name](*at)


def finish(norm, gg_in, gu_in, last, up_in, down_in, y_in, gg, gu, gd, total, sem):
    copies = [pltpu.make_async_copy(src, dst, sem.at[i]) for i, (src, dst) in enumerate(((gg_in, gg), (gu_in, gu)))]
    for cp in copies:
        cp.start()

    def rows(i, _):
        r = pl.ds(pl.multiple_of(i * 128, 128), 128)
        acc = last[r, :].astype(F32)
        for ref in (up_in, down_in, y_in):
            acc += ref[r, :].astype(F32)
        total[r, :] = (acc * norm).astype(BF16)
        return 0

    lax.fori_loop(0, total.shape[0] // 128, rows, 0)
    copies.append(pltpu.make_async_copy(total, gd, sem.at[2]))
    copies[-1].start()
    for cp in copies:
        cp.wait()


def shards(out_grad, gate_pre, up_pre, down_weight):
    TB, D = out_grad.shape
    TOK, FFD = gate_pre.shape
    BLK = down_weight.shape[1]
    n = len(ORDER)
    any_spec = pl.BlockSpec(memory_space=pl.ANY)
    dma = pltpu.SemaphoreType.DMA
    flops = 4 * TOK * D * FFD
    results = pl.pallas_call(
        kernel,
        out_shape=[pltpu.VMEM((TOK, FFD), BF16)] * 2 + [pltpu.VMEM((FFD, BLK), BF16)] * 4,
        in_specs=[any_spec] * 4,
        out_specs=[any_spec] * 6,
        scratch_shapes=[
            pltpu.VMEM((TOK, D), BF16),
            pltpu.VMEM((FFD, D), BF16),
            pltpu.VMEM((FFD, TOK), BF16),
            pltpu.VMEM((n, FFD, BLK), BF16),
            pltpu.VMEM((n, FFD, BLK), BF16),
            pltpu.VMEM((2, FFD, BLK), BF16),
            pltpu.VMEM((2, 2, FFD // 2, BLK), BF16),
            pltpu.VMEM((2, FFD, BLK), BF16),
            pltpu.VMEM((3, FFD - SPLIT2, BLK), BF16),
            pltpu.VMEM((TOK, BLK), F32),
            pltpu.VMEM((2, TOK, BLK), BF16),
            pltpu.VMEM((2, TOK, BLK), BF16),
            pltpu.VMEM((2, TOK, BLK), BF16),
            pltpu.VMEM((2, TOK, BLK), BF16),
            dma,
            dma,
            dma((2,)),
            dma,
            dma((n, 4)),
            dma((len(W_GROUPS),)),
            dma,
            dma((n,)),
            dma((2, 2)),
            dma((2,)),
            dma((3,)),
            dma,
            dma((2,)),
            dma,
            dma((2, 2)),
            dma((2, 2)),
            dma,
        ],
        compiler_params=pltpu.CompilerParams(
            collective_id=0, has_side_effects=True, vmem_limit_bytes=VMEM_LIMIT
        ),
        cost_estimate=pl.CostEstimate(flops=flops, bytes_accessed=40 << 20, transcendentals=0),
    )(out_grad, gate_pre, up_pre, down_weight)
    return pl.pallas_call(
        functools.partial(finish, 1.0 / math.sqrt(TOK * lax.axis_size("dp"))),
        out_shape=[jax.ShapeDtypeStruct(shape, BF16) for shape in ((TOK, FFD), (TOK, FFD), (FFD, BLK))],
        in_specs=[any_spec] * 2 + [pl.BlockSpec(memory_space=pltpu.VMEM)] * 4,
        out_specs=[any_spec] * 3,
        scratch_shapes=[pltpu.VMEM((FFD, BLK), BF16), dma((3,))],
        compiler_params=pltpu.CompilerParams(vmem_limit_bytes=2 << 20),
    )(*(pltpu.with_memory_space_constraint(a, pltpu.VMEM) for a in results))


def solution(mesh):
    return jax.shard_map(
        shards,
        mesh=mesh,
        in_specs=(P(("dp", "mp"), None), P("dp", "mp"), P("dp", "mp"), P("mp", "dp")),
        out_specs=(P("dp", "mp"), P("dp", "mp"), P("mp", "dp")),
        check_vma=False,
    )
```

```python
import functools
import math

import jax
import jax.numpy as jnp
from jax import lax
from jax.experimental import pallas as pl
from jax.experimental.pallas import tpu as pltpu
from jax.sharding import PartitionSpec as P

MESH = pl.DeviceIdType.MESH
F32 = jnp.float32
BF16 = jnp.bfloat16

ORDER = ((2, 1), (2, 0), (1, 1), (-1, 1), (1, 0), (-1, 0), (0, 1), (0, 0))
SLOT = {at: k for k, at in enumerate(ORDER)}
W_GROUPS = (
    ((-1, 0, 0), (1, 0, 1)), ((-1, 0, 1),), ((1, 0, 0),), ((2, 0, 0), (2, 0, 1)), ((0, 1, 0),), ((0, 1, 1),), ((0, 1, 2),),
    ((-1, 1, 0), (1, 1, 1)), ((-1, 1, 1), (-1, 1, 2)), ((1, 1, 0), (1, 1, 2)), ((2, 1, 0), (2, 1, 1), (2, 1, 2)),
)
SPLIT = 1152
SPLIT2 = 1280
FIRST = 1
VMEM_LIMIT = 51 << 20
SCHEDULE = (
    ("Wz", 0), ("O0", 1), ("O0", 3), ("O0", 0), ("H", 0), ("H", 1), ("Wz", 1), ("O0", 2), ("O1b", 3), ("Wy", 0),
    ("Wy", 1), ("O1b", 0), ("O1b", 1), ("O1a", 3), ("H", 2), ("O1a", 0), ("Wr", 0), ("O2", 0), ("Wy", 2), ("O2", 1),
    ("O1a", 2), ("H", 3), ("O2", 3), ("H", 4), ("H", 5), ("O1a", 1), ("O3", 0), ("Wp", 0), ("O1b", 2), ("Wp", 1),
    ("O0", 5), ("O0", 4), ("H", 6), ("T", 0), ("P", 0, 1), ("O3", 1), ("O0", 6), ("PY", 0), ("Wc", 0), ("O0", 7),
    ("Ws", 0, 1), ("T", 1), ("O2", 2), ("P", 0, 0), ("O1b", 5), ("Wq", 2), ("Ws", 0, 0), ("O3", 3), ("Wr", 1),
    ("O1b", 4), ("T", 3), ("P", 1, 0), ("Wq", -1), ("O1a", 5), ("O3", 2), ("P", 1, 1), ("O1b", 6), ("T", 2),
    ("Ws", 2, 0), ("O2", 5), ("Wq", 1), ("O2", 4), ("O1a", 4), ("Ws", -1, 0), ("P", 2, 1), ("O1b", 7), ("P", 3, 1),
    ("O1a", 6), ("Ws", 1, 0), ("PY", 3), ("Wc", 2), ("PY", 2), ("P", 3, 0), ("O3", 5), ("O2", 6), ("Ws", 2, 1),
    ("O1a", 7), ("T", 5), ("O3", 4), ("T", 4), ("P", 2, 0), ("Wc", -1), ("O2", 7), ("P", 5, 0), ("O3", 6),
    ("Ws", -1, 1), ("T", 6), ("Wc", 1), ("O3", 7), ("Ws", 1, 1), ("T", 7), ("P", 4, 0), ("PY", 6), ("WD",), ("D", 0),
    ("D", 1), ("P", 6, 1), ("P", 4, 1), ("D", 2), ("P", 5, 1), ("P", 6, 0), ("Z", 0), ("D", 3), ("D", 4), ("D", 5),
    ("D", 6), ("Z", 1),
)


def kernel(
    og, gp, up, w, gg, gu, last, up_in, down_in, y_in,
    o_all, w_all, h_t, own, pre, snd, half_in, full_in, y_early, acc, gbuf, ubuf, ggbuf, gubuf,
    o_send, w_send, t_send, r_send, o_recv, w_recv, wc_recv, t_recv, half_recv, full_recv, y_recv, end_recv,
    o_local, w_local, in_sem, out_sem, last_sem,
):
    TB = og.shape[0]
    BLK = w.shape[1]
    FFD = w.shape[0]
    TOK = gp.shape[0]
    HALF = FFD // 2
    TH = TB // 2
    NT = FFD // BLK

    dp = lax.axis_index("dp")
    mp = lax.axis_index("mp")
    z, yl, c = dp // 4, (dp // 2) % 2, dp % 2
    yh, x = mp // 4, mp % 4

    def dev(dz=0, o=0, cc=0, h=0, dx=0):
        a = ((z + dz + 4) % 4) * 4 + ((yl + o) % 2) * 2 + (c + cc) % 2
        b = ((yh + h) % 2) * 4 + (x + dx + 4) % 4
        return (a, b)

    ZP, ZM, YP, CP = dev(dz=1), dev(dz=-1), dev(o=1), dev(cc=1)
    HP, XP, XM = dev(h=1), dev(dx=1), dev(dx=-1)

    def send(src, dst, ss, rs, to):
        cp = pltpu.make_async_remote_copy(src, dst, ss, rs, device_id=to, device_id_type=MESH)
        cp.start()
        return cp

    def arrived(like, rs):
        pltpu.make_async_remote_copy(like, like, o_send, rs, device_id=CP, device_id_type=MESH).wait_recv()

    def sent(like, ss):
        pltpu.make_async_remote_copy(like, like, ss, end_recv, device_id=CP, device_id_type=MESH).wait_send()

    barrier = pltpu.get_barrier_semaphore()
    for to in (ZP, ZM, YP, CP, HP, XP, XM):
        pl.semaphore_signal(barrier, inc=1, device_id=to, device_id_type=MESH)

    def tile_in(n, slot):
        cols = pl.ds(pl.multiple_of(n * BLK, BLK), BLK)
        return (
            pltpu.make_async_copy(gp.at[:, cols], gbuf.at[slot], in_sem.at[slot, 0]),
            pltpu.make_async_copy(up.at[:, cols], ubuf.at[slot], in_sem.at[slot, 1]),
        )

    def tile_out(n, slot):
        cols = pl.ds(pl.multiple_of(n * BLK, BLK), BLK)
        return (
            pltpu.make_async_copy(ggbuf.at[slot], gg.at[:, cols], out_sem.at[slot, 0]),
            pltpu.make_async_copy(gubuf.at[slot], gu.at[:, cols], out_sem.at[slot, 1]),
        )

    def o_cols(k):
        return pl.ds(k * 2 * BLK, 2 * BLK)

    def o_rows(h, dx, part=None):
        base = (((yh + h) % 2) * 4 + (x + dx + 4) % 4) * TB
        if part is None:
            return pl.ds(pl.multiple_of(base, TB), TB)
        return pl.ds(pl.multiple_of(base + part * TH, TH), TH)

    def w_cols(k, cc):
        return pl.ds((2 * k + cc) * BLK, BLK)

    w_own = pltpu.make_async_copy(w, w_all.at[:, w_cols(SLOT[0, 0], 0)], w_local)
    w_own.start()
    for k, (dz, o) in enumerate(ORDER):
        for cc in range(2):
            d = ((z + dz + 4) % 4) * 4 + ((yl + o) % 2) * 2 + (c + cc) % 2
            cp = pltpu.make_async_copy(
                og.at[:, pl.ds(pl.multiple_of(d * BLK, BLK), BLK)],
                o_all.at[o_rows(0, 0), pl.ds((2 * k + cc) * BLK, BLK)],
                o_local.at[0 if k == FIRST else 1],
            )
            cp.start()
    for slot in range(2):
        for cp in tile_in(slot, slot):
            cp.start()

    pl.semaphore_wait(barrier, 7)

    def w_part(dz, o, part):
        if o == 0:
            rows = pl.ds(part * HALF, HALF)
        elif part < 2:
            rows = pl.ds(part * (SPLIT // 2), SPLIT // 2)
        else:
            rows = pl.ds(SPLIT, FFD - SPLIT)
        return w_all.at[rows, w_cols(SLOT[dz, o], 0)]

    def w_size(o, part):
        return HALF if o == 0 else SPLIT // 2 if part < 2 else FFD - SPLIT

    w_group = {part: i for i, group in enumerate(W_GROUPS) for part in group}
    w_seen = set()

    def w_to(src, dz, o, part, to):
        send(src, w_part(dz, o, part), w_send, w_recv.at[w_group[dz, o, part]], to)

    def w_got(dz, o, part):
        i = w_group[dz, o, part]
        if i not in w_seen:
            w_seen.add(i)
            rows = sum(w_size(o, part) for _, o, part in W_GROUPS[i])
            arrived(w_all.at[pl.ds(0, rows), pl.ds(0, BLK)], w_recv.at[i])

    def Wz(p):
        w_to(w.at[pl.ds(p * HALF, HALF), :], -1, 0, p, ZP)
        w_to(w.at[pl.ds((1 - p) * HALF, HALF), :], 1, 0, 1 - p, ZM)

    def Wy(p):
        rows = (pl.ds(0, SPLIT // 2), pl.ds(SPLIT // 2, SPLIT // 2), pl.ds(SPLIT, FFD - SPLIT))[p]
        w_to(w.at[rows, :], 0, 1, p, YP)

    def Wr(o):
        w_got(-1, o, 0)
        w_to(w_part(-1, o, 0), 2, o, 0, ZP)
        w_got(1, o, 1)
        w_to(w_part(1, o, 1), 2, o, 1, ZM)

    def Wp(p):
        w_got(0, 1, p)
        for dz, to in ((-1, ZP), (1, ZM)) if p == 0 else ((1, ZM), (-1, ZP)):
            w_to(w_part(0, 1, p), dz, 1, p, to)

    def Wq(dz):
        w_got(dz, 0, 0)
        w_got(dz, 0, 1)
        src = w_all.at[pl.ds(SPLIT, FFD - SPLIT), w_cols(SLOT[dz, 0], 0)]
        w_to(src, dz, 1, 2, YP)

    def Wc(dz):
        for p in range(3):
            w_got(dz, 1, p)

    def Ws(dz, o):
        k = SLOT[dz, o]
        if (dz, o) == (0, 0):
            w_own.wait()
        send(w_all.at[:, w_cols(k, 0)], w_all.at[:, w_cols(k, 1)], w_send, wc_recv, CP)

    def WD():
        arrived(w_all.at[:, pl.ds(0, len(ORDER) * BLK)], wc_recv)

    def o_to(k, h, dx, part, kind, to):
        ref = o_all.at[o_rows(h, dx, part), o_cols(k)]
        send(ref, ref, o_send, o_recv.at[k, kind], to)

    def o_got(k, rows, kind):
        arrived(o_all.at[pl.ds(0, rows), o_cols(k)], o_recv.at[k, kind])

    o_ready = set()

    def O0(k):
        i = 0 if k == FIRST else 1
        if i not in o_ready:
            o_ready.add(i)
            mine = o_all.at[o_rows(0, 0), pl.ds(0, (2 if i == 0 else 14) * BLK)]
            pltpu.make_async_copy(mine, mine, o_local.at[i]).wait()
        o_to(k, 0, 0, None, 0, HP)
        o_to(k, 0, 0, None, 1, XP)
        o_to(k, 0, 0, None, 1, XM)

    def O1a(k):
        o_got(k, 2 * TB, 1)
        o_to(k, 0, -1, 0, 3, XP)
        o_to(k, 0, 1, 1, 3, XM)

    def O1b(k):
        o_got(k, TB, 0)
        o_to(k, 1, 0, None, 2, XP)
        o_to(k, 1, 0, None, 2, XM)

    def O2(k):
        o_got(k, 2 * TB, 2)
        o_to(k, 1, -1, 0, 3, XP)
        o_to(k, 1, 1, 1, 3, XM)

    def O3(k):
        o_got(k, 2 * TB, 3)

    def H(n):
        slot = n % 2
        for cp in tile_in(n, slot):
            cp.wait()

        def rows(i, _):
            r = pl.ds(pl.multiple_of(i * 128, 128), 128)
            g = gbuf[slot, r, :].astype(F32)
            u = ubuf[slot, r, :].astype(F32)
            hid = g * jax.nn.sigmoid(g) * u
            h_t[pl.ds(pl.multiple_of(n * BLK, BLK), BLK), r] = hid.T.astype(BF16)
            return 0

        lax.fori_loop(0, TOK // 128, rows, 0)

        if n + 2 < NT:
            for cp in tile_in(n + 2, slot):
                cp.start()
        elif n == NT - 1:
            for first in range(2):
                for cp in tile_in(first, first):
                    cp.start()

    def term(k, cc, dst):
        def rows(i, _):
            r = pl.ds(pl.multiple_of(i * HALF, HALF), HALF)
            dst[r, :] = jnp.dot(
                h_t[r, :], o_all[:, pl.ds((2 * k + cc) * BLK, BLK)], preferred_element_type=F32
            ).astype(BF16)
            return 0

        lax.fori_loop(0, 2, rows, 0)

    t_copies = {}

    def T(k):
        slot = k % 2
        if k >= 2:
            t_copies.pop(k - 2).wait_send()
        term(k, 1, snd.at[slot])
        t_copies[k] = send(snd.at[slot], pre.at[k], t_send.at[slot], t_recv.at[k], CP)
        term(k, 0, own.at[k])

    def row_part(o, p):
        if o == 0:
            return p * HALF, HALF
        return (p * (SPLIT2 // 2), SPLIT2 // 2) if p < 2 else (SPLIT2, FFD - SPLIT2)

    def add(k, at, size, others):
        step = 32
        others = [(pre.at[k], 0, FFD), *others]
        cuts = {at, at + size}
        for _, first, many in others:
            cuts |= {row for row in (first, first + many) if at < row < at + size}
        cuts = sorted(cuts)
        for low, high in zip(cuts, cuts[1:]):
            inside = [(ref, first) for ref, first, many in others if first <= low and high <= first + many]

            def rows(i, _, low=low, inside=inside):
                r = pl.ds(pl.multiple_of(low + i * step, step), step)
                total = own[k, r, :].astype(F32)
                for ref, first in inside:
                    total += ref[pl.ds(pl.multiple_of(low - first + i * step, step), step), :].astype(F32)
                own[k, r, :] = total.astype(BF16)
                return 0

            lax.fori_loop(0, (high - low) // step, rows, 0)

    seen = set()
    last_copies = []

    def t_got(k):
        if k not in seen:
            seen.add(k)
            arrived(pre.at[k], t_recv.at[k])

    def like(rows):
        return pre.at[0, pl.ds(0, rows), :]

    def y_to(k, dz, p):
        at, size = row_part(1, p)
        src = own.at[k, pl.ds(at, size), :]
        if dz == 0:
            send(src, y_in.at[pl.ds(at, size), :], r_send, end_recv, YP)
        else:
            i = (2, 1, -1).index(dz)
            send(src, y_early.at[i], r_send, y_recv.at[i], YP)

    def PY(k):
        t_got(k)
        at, size = row_part(1, 2)
        add(k, at, size, [])
        y_to(k, ORDER[k][0], 2)

    def Pk(k, p):
        dz, o = ORDER[k]
        at, size = row_part(o, p)
        rows = pl.ds(at, size)
        blk = own.at[k, rows, :]
        t_got(k)
        others = []
        if o == 0 and p == 1:
            i = (2, 1, -1).index(dz)
            arrived(y_early.at[i], y_recv.at[i])
            others.append((y_early.at[i], SPLIT2, FFD - SPLIT2))
        if dz == 2:
            add(k, at, size, others)
            send(blk, half_in.at[o, p, pl.ds(0, size), :], r_send, half_recv.at[o, p], (ZP, ZM)[p])
        elif dz:
            side = 0 if dz == 1 else 1
            if p == side:
                ref = half_in.at[o, p, pl.ds(0, size), :]
                arrived(ref, half_recv.at[o, p])
                others.append((ref, at, size))
            add(k, at, size, others)
            if o == 1:
                send(blk, full_in.at[side, rows, :], r_send, full_recv.at[p], (ZP, ZM)[side])
            else:
                send(blk, (up_in, down_in)[side].at[rows, :], r_send, end_recv, (ZP, ZM)[side])
        else:
            arrived(like(2 * size), full_recv.at[p])
            add(k, at, size, [(full_in.at[side], 0, FFD) for side in range(2)])
            y_to(k, 0, p)

    def Z(p):
        k = SLOT[0, 0]
        if p == 0:
            t_got(k)
            add(k, 0, FFD, [])
            cp = pltpu.make_async_copy(own.at[k], last, last_sem)
            cp.start()
            last_copies.append(cp)
            return
        for cp in tile_out(NT - 2, (NT - 2) % 2) + tile_out(NT - 1, (NT - 1) % 2) + tuple(last_copies):
            cp.wait()
        blocks = len(ORDER)
        sent(o_all.at[pl.ds(0, 7 * TB), :], o_send)
        sent(w_all.at[:, pl.ds(0, (2 * blocks - 1) * BLK)], w_send)
        for cp in t_copies.values():
            cp.wait_send()
        sent(pre.at[pl.ds(0, blocks - 1)], r_send)
        arrived(pre.at[pl.ds(0, 3)], end_recv)

    def D(n):
        slot = n % 2

        def mm(i, _):
            r = pl.ds(pl.multiple_of(i * 512, 512), 512)
            acc[r, :] = lax.dot_general(
                o_all[r, :],
                w_all[pl.ds(pl.multiple_of(n * BLK, BLK), BLK), :],
                (((1,), (1,)), ((), ())),
                preferred_element_type=F32,
            )
            return 0

        lax.fori_loop(0, TOK // 512, mm, 0)
        for cp in tile_in(n, slot):
            cp.wait()

        if n >= 2:
            for cp in tile_out(n - 2, slot):
                cp.wait()

        def rows(i, _):
            r = pl.ds(pl.multiple_of(i * 64, 64), 64)
            g = gbuf[slot, r, :].astype(F32)
            u = ubuf[slot, r, :].astype(F32)
            d = acc[r, :]
            s = jax.nn.sigmoid(g)
            ggbuf[slot, r, :] = (d * u * s * (1.0 + g * (1.0 - s))).astype(BF16)
            gubuf[slot, r, :] = (d * (g * s)).astype(BF16)
            return 0

        lax.fori_loop(0, TOK // 64, rows, 0)
        for cp in tile_out(n, slot):
            cp.start()
        if n + 2 < NT:
            for cp in tile_in(n + 2, slot):
                cp.start()

    tasks = dict(
        O0=O0, O1a=O1a, O1b=O1b, O2=O2, O3=O3, H=H, T=T, P=Pk, PY=PY, Z=Z, D=D,
        Wz=Wz, Wy=Wy, Wr=Wr, Wp=Wp, Wq=Wq, Wc=Wc, Ws=Ws, WD=WD,
    )
    for name, *at in SCHEDULE:
        tasks[name](*at)


def finish(norm, gg_in, gu_in, last, up_in, down_in, y_in, gg, gu, gd, total, sem):
    copies = [pltpu.make_async_copy(src, dst, sem.at[i]) for i, (src, dst) in enumerate(((gg_in, gg), (gu_in, gu)))]
    for cp in copies:
        cp.start()

    def rows(i, _):
        r = pl.ds(pl.multiple_of(i * 128, 128), 128)
        acc = last[r, :].astype(F32)
        for ref in (up_in, down_in, y_in):
            acc += ref[r, :].astype(F32)
        total[r, :] = (acc * norm).astype(BF16)
        return 0

    lax.fori_loop(0, total.shape[0] // 128, rows, 0)
    copies.append(pltpu.make_async_copy(total, gd, sem.at[2]))
    copies[-1].start()
    for cp in copies:
        cp.wait()


def shards(out_grad, gate_pre, up_pre, down_weight):
    TB, D = out_grad.shape
    TOK, FFD = gate_pre.shape
    BLK = down_weight.shape[1]
    n = len(ORDER)
    any_spec = pl.BlockSpec(memory_space=pl.ANY)
    dma = pltpu.SemaphoreType.DMA
    flops = 4 * TOK * D * FFD
    results = pl.pallas_call(
        kernel,
        out_shape=[pltpu.VMEM((TOK, FFD), BF16)] * 2 + [pltpu.VMEM((FFD, BLK), BF16)] * 4,
        in_specs=[any_spec] * 4,
        out_specs=[any_spec] * 6,
        scratch_shapes=[
            pltpu.VMEM((TOK, D), BF16),
            pltpu.VMEM((FFD, D), BF16),
            pltpu.VMEM((FFD, TOK), BF16),
            pltpu.VMEM((n, FFD, BLK), BF16),
            pltpu.VMEM((n, FFD, BLK), BF16),
            pltpu.VMEM((2, FFD, BLK), BF16),
            pltpu.VMEM((2, 2, FFD // 2, BLK), BF16),
            pltpu.VMEM((2, FFD, BLK), BF16),
            pltpu.VMEM((3, FFD - SPLIT2, BLK), BF16),
            pltpu.VMEM((TOK, BLK), F32),
            pltpu.VMEM((2, TOK, BLK), BF16),
            pltpu.VMEM((2, TOK, BLK), BF16),
            pltpu.VMEM((2, TOK, BLK), BF16),
            pltpu.VMEM((2, TOK, BLK), BF16),
            dma,
            dma,
            dma((2,)),
            dma,
            dma((n, 4)),
            dma((len(W_GROUPS),)),
            dma,
            dma((n,)),
            dma((2, 2)),
            dma((2,)),
            dma((3,)),
            dma,
            dma((2,)),
            dma,
            dma((2, 2)),
            dma((2, 2)),
            dma,
        ],
        compiler_params=pltpu.CompilerParams(
            collective_id=0, has_side_effects=True, vmem_limit_bytes=VMEM_LIMIT
        ),
        cost_estimate=pl.CostEstimate(flops=flops, bytes_accessed=40 << 20, transcendentals=0),
    )(out_grad, gate_pre, up_pre, down_weight)
    return pl.pallas_call(
        functools.partial(finish, 1.0 / math.sqrt(TOK * lax.axis_size("dp"))),
        out_shape=[jax.ShapeDtypeStruct(shape, BF16) for shape in ((TOK, FFD), (TOK, FFD), (FFD, BLK))],
        in_specs=[any_spec] * 2 + [pl.BlockSpec(memory_space=pltpu.VMEM)] * 4,
        out_specs=[any_spec] * 3,
        scratch_shapes=[pltpu.VMEM((FFD, BLK), BF16), dma((3,))],
        compiler_params=pltpu.CompilerParams(vmem_limit_bytes=2 << 20),
    )(*(pltpu.with_memory_space_constraint(a, pltpu.VMEM) for a in results))


def solution(mesh):
    return jax.shard_map(
        shards,
        mesh=mesh,
        in_specs=(P(("dp", "mp"), None), P("dp", "mp"), P("dp", "mp"), P("mp", "dp")),
        out_specs=(P("dp", "mp"), P("dp", "mp"), P("mp", "dp")),
        check_vma=False,
    )
```

```python
import functools
import math

import jax
import jax.numpy as jnp
from jax import lax
from jax.experimental import pallas as pl
from jax.experimental.pallas import tpu as pltpu
from jax.sharding import PartitionSpec as P

MESH = pl.DeviceIdType.MESH
F32 = jnp.float32
BF16 = jnp.bfloat16

ORDER = ((2, 1), (2, 0), (1, 1), (-1, 1), (1, 0), (-1, 0), (0, 1), (0, 0))
SLOT = {at: k for k, at in enumerate(ORDER)}
W_GROUPS = (
    ((-1, 0, 0), (1, 0, 1)), ((-1, 0, 1),), ((1, 0, 0),), ((2, 0, 0), (2, 0, 1)), ((0, 1, 0),), ((0, 1, 1),), ((0, 1, 2),),
    ((-1, 1, 0), (1, 1, 1)), ((-1, 1, 1), (-1, 1, 2)), ((1, 1, 0), (1, 1, 2)), ((2, 1, 0), (2, 1, 1), (2, 1, 2)),
)
SPLIT = 1152
SPLIT2 = 1280
FIRST = 1
VMEM_LIMIT = 51 << 20
SCHEDULE = (
    ("Wz", 0), ("O0", 1), ("O0", 3), ("O0", 0), ("H", 0), ("H", 1), ("Wz", 1), ("O0", 2), ("O1b", 3), ("Wy", 0),
    ("Wy", 1), ("O1b", 0), ("O1b", 1), ("O1a", 3), ("H", 2), ("O1a", 0), ("Wr", 0), ("O2", 0), ("Wy", 2), ("O2", 1),
    ("O1a", 2), ("H", 3), ("O2", 3), ("H", 4), ("H", 5), ("O1a", 1), ("O3", 0), ("Wp", 0), ("O1b", 2), ("Wp", 1),
    ("O0", 5), ("O0", 4), ("H", 6), ("T", 0), ("P", 0, 1), ("O3", 1), ("O0", 6), ("PY", 0), ("Wc", 0), ("O0", 7),
    ("Ws", 0, 1), ("T", 1), ("O2", 2), ("P", 0, 0), ("O1b", 5), ("Wq", 2), ("Ws", 0, 0), ("O3", 3), ("Wr", 1),
    ("O1b", 4), ("T", 3), ("P", 1, 0), ("Wq", -1), ("O1a", 5), ("O3", 2), ("P", 1, 1), ("O1b", 6), ("T", 2),
    ("Ws", 2, 0), ("O2", 5), ("Wq", 1), ("O2", 4), ("O1a", 4), ("Ws", -1, 0), ("P", 2, 1), ("O1b", 7), ("P", 3, 1),
    ("O1a", 6), ("Ws", 1, 0), ("PY", 3), ("Wc", 2), ("PY", 2), ("P", 3, 0), ("O3", 5), ("O2", 6), ("Ws", 2, 1),
    ("O1a", 7), ("T", 5), ("O3", 4), ("T", 4), ("P", 2, 0), ("Wc", -1), ("O2", 7), ("P", 5, 0), ("O3", 6),
    ("Ws", -1, 1), ("T", 6), ("Wc", 1), ("O3", 7), ("Ws", 1, 1), ("T", 7), ("P", 4, 0), ("PY", 6), ("WD",), ("D", 0),
    ("D", 1), ("P", 6, 1), ("P", 4, 1), ("D", 2), ("P", 5, 1), ("P", 6, 0), ("Z", 0), ("D", 3), ("D", 4), ("D", 5),
    ("D", 6), ("Z", 1),
)


def kernel(
    og, gp, up, w, gg, gu, last, up_in, down_in, y_in,
    o_all, w_all, h_t, own, pre, snd, half_in, full_in, y_early, acc, gbuf, ubuf, ggbuf, gubuf,
    o_send, w_send, t_send, r_send, o_recv, w_recv, wc_recv, t_recv, half_recv, full_recv, y_recv, end_recv,
    o_local, w_local, in_sem, out_sem, last_sem,
):
    TB = og.shape[0]
    BLK = w.shape[1]
    FFD = w.shape[0]
    TOK = gp.shape[0]
    HALF = FFD // 2
    TH = TB // 2
    NT = FFD // BLK

    dp = lax.axis_index("dp")
    mp = lax.axis_index("mp")
    z, yl, c = dp // 4, (dp // 2) % 2, dp % 2
    yh, x = mp // 4, mp % 4

    def dev(dz=0, o=0, cc=0, h=0, dx=0):
        a = ((z + dz + 4) % 4) * 4 + ((yl + o) % 2) * 2 + (c + cc) % 2
        b = ((yh + h) % 2) * 4 + (x + dx + 4) % 4
        return (a, b)

    ZP, ZM, YP, CP = dev(dz=1), dev(dz=-1), dev(o=1), dev(cc=1)
    HP, XP, XM = dev(h=1), dev(dx=1), dev(dx=-1)

    def send(src, dst, ss, rs, to):
        cp = pltpu.make_async_remote_copy(src, dst, ss, rs, device_id=to, device_id_type=MESH)
        cp.start()
        return cp

    def arrived(like, rs):
        pltpu.make_async_remote_copy(like, like, o_send, rs, device_id=CP, device_id_type=MESH).wait_recv()

    def sent(like, ss):
        pltpu.make_async_remote_copy(like, like, ss, end_recv, device_id=CP, device_id_type=MESH).wait_send()

    barrier = pltpu.get_barrier_semaphore()
    for to in (ZP, ZM, YP, CP, HP, XP, XM):
        pl.semaphore_signal(barrier, inc=1, device_id=to, device_id_type=MESH)

    def tile_in(n, slot):
        cols = pl.ds(pl.multiple_of(n * BLK, BLK), BLK)
        return (
            pltpu.make_async_copy(gp.at[:, cols], gbuf.at[slot], in_sem.at[slot]),
            pltpu.make_async_copy(up.at[:, cols], ubuf.at[slot], in_sem.at[slot]),
        )

    def both(buf, sem):
        pltpu.make_async_copy(buf, buf, sem).wait()

    def tile_out(n, slot):
        cols = pl.ds(pl.multiple_of(n * BLK, BLK), BLK)
        return (
            pltpu.make_async_copy(ggbuf.at[slot], gg.at[:, cols], out_sem.at[slot]),
            pltpu.make_async_copy(gubuf.at[slot], gu.at[:, cols], out_sem.at[slot]),
        )

    def o_cols(k):
        return pl.ds(k * 2 * BLK, 2 * BLK)

    def o_rows(h, dx, part=None):
        base = (((yh + h) % 2) * 4 + (x + dx + 4) % 4) * TB
        if part is None:
            return pl.ds(pl.multiple_of(base, TB), TB)
        return pl.ds(pl.multiple_of(base + part * TH, TH), TH)

    def w_cols(k, cc):
        return pl.ds((2 * k + cc) * BLK, BLK)

    w_own = pltpu.make_async_copy(w, w_all.at[:, w_cols(SLOT[0, 0], 0)], w_local)
    w_own.start()
    for k, (dz, o) in enumerate(ORDER):
        for cc in range(2):
            d = ((z + dz + 4) % 4) * 4 + ((yl + o) % 2) * 2 + (c + cc) % 2
            cp = pltpu.make_async_copy(
                og.at[:, pl.ds(pl.multiple_of(d * BLK, BLK), BLK)],
                o_all.at[o_rows(0, 0), pl.ds((2 * k + cc) * BLK, BLK)],
                o_local.at[0 if k == FIRST else 1],
            )
            cp.start()
    for slot in range(2):
        for cp in tile_in(slot, slot):
            cp.start()

    pl.semaphore_wait(barrier, 7)

    def w_part(dz, o, part):
        if o == 0:
            rows = pl.ds(part * HALF, HALF)
        elif part < 2:
            rows = pl.ds(part * (SPLIT // 2), SPLIT // 2)
        else:
            rows = pl.ds(SPLIT, FFD - SPLIT)
        return w_all.at[rows, w_cols(SLOT[dz, o], 0)]

    def w_size(o, part):
        return HALF if o == 0 else SPLIT // 2 if part < 2 else FFD - SPLIT

    w_group = {part: i for i, group in enumerate(W_GROUPS) for part in group}
    w_seen = set()

    def w_to(src, dz, o, part, to):
        send(src, w_part(dz, o, part), w_send, w_recv.at[w_group[dz, o, part]], to)

    def w_got(dz, o, part):
        i = w_group[dz, o, part]
        if i not in w_seen:
            w_seen.add(i)
            rows = sum(w_size(o, part) for _, o, part in W_GROUPS[i])
            arrived(w_all.at[pl.ds(0, rows), pl.ds(0, BLK)], w_recv.at[i])

    def Wz(p):
        w_to(w.at[pl.ds(p * HALF, HALF), :], -1, 0, p, ZP)
        w_to(w.at[pl.ds((1 - p) * HALF, HALF), :], 1, 0, 1 - p, ZM)

    def Wy(p):
        rows = (pl.ds(0, SPLIT // 2), pl.ds(SPLIT // 2, SPLIT // 2), pl.ds(SPLIT, FFD - SPLIT))[p]
        w_to(w.at[rows, :], 0, 1, p, YP)

    def Wr(o):
        w_got(-1, o, 0)
        w_to(w_part(-1, o, 0), 2, o, 0, ZP)
        w_got(1, o, 1)
        w_to(w_part(1, o, 1), 2, o, 1, ZM)

    def Wp(p):
        w_got(0, 1, p)
        for dz, to in ((-1, ZP), (1, ZM)) if p == 0 else ((1, ZM), (-1, ZP)):
            w_to(w_part(0, 1, p), dz, 1, p, to)

    def Wq(dz):
        w_got(dz, 0, 0)
        w_got(dz, 0, 1)
        src = w_all.at[pl.ds(SPLIT, FFD - SPLIT), w_cols(SLOT[dz, 0], 0)]
        w_to(src, dz, 1, 2, YP)

    def Wc(dz):
        for p in range(3):
            w_got(dz, 1, p)

    def Ws(dz, o):
        k = SLOT[dz, o]
        if (dz, o) == (0, 0):
            w_own.wait()
        send(w_all.at[:, w_cols(k, 0)], w_all.at[:, w_cols(k, 1)], w_send, wc_recv, CP)

    def WD():
        arrived(w_all.at[:, pl.ds(0, len(ORDER) * BLK)], wc_recv)

    def o_to(k, h, dx, part, kind, to):
        ref = o_all.at[o_rows(h, dx, part), o_cols(k)]
        send(ref, ref, o_send, o_recv.at[k, kind], to)

    def o_got(k, rows, kind):
        arrived(o_all.at[pl.ds(0, rows), o_cols(k)], o_recv.at[k, kind])

    o_ready = set()

    def O0(k):
        i = 0 if k == FIRST else 1
        if i not in o_ready:
            o_ready.add(i)
            mine = o_all.at[o_rows(0, 0), pl.ds(0, (2 if i == 0 else 14) * BLK)]
            pltpu.make_async_copy(mine, mine, o_local.at[i]).wait()
        o_to(k, 0, 0, None, 0, HP)
        o_to(k, 0, 0, None, 1, XP)
        o_to(k, 0, 0, None, 1, XM)

    def O1a(k):
        o_got(k, 2 * TB, 1)
        o_to(k, 0, -1, 0, 3, XP)
        o_to(k, 0, 1, 1, 3, XM)

    def O1b(k):
        o_got(k, TB, 0)
        o_to(k, 1, 0, None, 2, XP)
        o_to(k, 1, 0, None, 2, XM)

    def O2(k):
        o_got(k, 2 * TB, 2)
        o_to(k, 1, -1, 0, 3, XP)
        o_to(k, 1, 1, 1, 3, XM)

    def O3(k):
        o_got(k, 2 * TB, 3)

    def H(n):
        slot = n % 2
        both(gbuf, in_sem.at[slot])

        def rows(i, _):
            r = pl.ds(pl.multiple_of(i * 128, 128), 128)
            g = gbuf[slot, r, :].astype(F32)
            u = ubuf[slot, r, :].astype(F32)
            hid = g * jax.nn.sigmoid(g) * u
            h_t[pl.ds(pl.multiple_of(n * BLK, BLK), BLK), r] = hid.T.astype(BF16)
            return 0

        lax.fori_loop(0, TOK // 128, rows, 0)

        if n + 2 < NT:
            for cp in tile_in(n + 2, slot):
                cp.start()
        elif n == NT - 1:
            for first in range(2):
                for cp in tile_in(first, first):
                    cp.start()

    def term(k, cc, dst):
        def rows(i, _):
            r = pl.ds(pl.multiple_of(i * HALF, HALF), HALF)
            dst[r, :] = jnp.dot(
                h_t[r, :], o_all[:, pl.ds((2 * k + cc) * BLK, BLK)], preferred_element_type=F32
            ).astype(BF16)
            return 0

        lax.fori_loop(0, 2, rows, 0)

    t_copies = {}

    def T(k):
        slot = k % 2
        if k >= 2:
            t_copies.pop(k - 2).wait_send()
        term(k, 1, snd.at[slot])
        t_copies[k] = send(snd.at[slot], pre.at[k], t_send.at[slot], t_recv.at[k], CP)
        term(k, 0, own.at[k])

    def row_part(o, p):
        if o == 0:
            return p * HALF, HALF
        return (p * (SPLIT2 // 2), SPLIT2 // 2) if p < 2 else (SPLIT2, FFD - SPLIT2)

    def add(k, at, size, others):
        step = 32
        others = [(pre.at[k], 0, FFD), *others]
        cuts = {at, at + size}
        for _, first, many in others:
            cuts |= {row for row in (first, first + many) if at < row < at + size}
        cuts = sorted(cuts)
        for low, high in zip(cuts, cuts[1:]):
            inside = [(ref, first) for ref, first, many in others if first <= low and high <= first + many]

            def rows(i, _, low=low, inside=inside):
                r = pl.ds(pl.multiple_of(low + i * step, step), step)
                total = own[k, r, :].astype(F32)
                for ref, first in inside:
                    total += ref[pl.ds(pl.multiple_of(low - first + i * step, step), step), :].astype(F32)
                own[k, r, :] = total.astype(BF16)
                return 0

            lax.fori_loop(0, (high - low) // step, rows, 0)

    seen = set()
    last_copies = []

    def t_got(k):
        if k not in seen:
            seen.add(k)
            arrived(pre.at[k], t_recv.at[k])

    def like(rows):
        return pre.at[0, pl.ds(0, rows), :]

    def y_to(k, dz, p):
        at, size = row_part(1, p)
        src = own.at[k, pl.ds(at, size), :]
        if dz == 0:
            send(src, y_in.at[pl.ds(at, size), :], r_send, end_recv, YP)
        else:
            i = (2, 1, -1).index(dz)
            send(src, y_early.at[i], r_send, y_recv.at[i], YP)

    def PY(k):
        t_got(k)
        at, size = row_part(1, 2)
        add(k, at, size, [])
        y_to(k, ORDER[k][0], 2)

    def Pk(k, p):
        dz, o = ORDER[k]
        at, size = row_part(o, p)
        rows = pl.ds(at, size)
        blk = own.at[k, rows, :]
        t_got(k)
        others = []
        if o == 0 and p == 1:
            i = (2, 1, -1).index(dz)
            arrived(y_early.at[i], y_recv.at[i])
            others.append((y_early.at[i], SPLIT2, FFD - SPLIT2))
        if dz == 2:
            add(k, at, size, others)
            send(blk, half_in.at[o, p, pl.ds(0, size), :], r_send, half_recv.at[o, p], (ZP, ZM)[p])
        elif dz:
            side = 0 if dz == 1 else 1
            if p == side:
                ref = half_in.at[o, p, pl.ds(0, size), :]
                arrived(ref, half_recv.at[o, p])
                others.append((ref, at, size))
            add(k, at, size, others)
            if o == 1:
                send(blk, full_in.at[side, rows, :], r_send, full_recv.at[p], (ZP, ZM)[side])
            else:
                send(blk, (up_in, down_in)[side].at[rows, :], r_send, end_recv, (ZP, ZM)[side])
        else:
            arrived(like(2 * size), full_recv.at[p])
            add(k, at, size, [(full_in.at[side], 0, FFD) for side in range(2)])
            y_to(k, 0, p)

    def Z(p):
        k = SLOT[0, 0]
        if p == 0:
            t_got(k)
            add(k, 0, FFD, [])
            cp = pltpu.make_async_copy(own.at[k], last, last_sem)
            cp.start()
            last_copies.append(cp)
            return
        for slot in range(2):
            both(ggbuf, out_sem.at[slot])
        for cp in last_copies:
            cp.wait()
        blocks = len(ORDER)
        sent(o_all.at[pl.ds(0, 7 * TB), :], o_send)
        sent(w_all.at[:, pl.ds(0, (2 * blocks - 1) * BLK)], w_send)
        for cp in t_copies.values():
            cp.wait_send()
        sent(pre.at[pl.ds(0, blocks - 1)], r_send)
        arrived(pre.at[pl.ds(0, 3)], end_recv)

    def D(n):
        slot = n % 2

        def mm(i, _):
            r = pl.ds(pl.multiple_of(i * 512, 512), 512)
            acc[r, :] = lax.dot_general(
                o_all[r, :],
                w_all[pl.ds(pl.multiple_of(n * BLK, BLK), BLK), :],
                (((1,), (1,)), ((), ())),
                preferred_element_type=F32,
            )
            return 0

        lax.fori_loop(0, TOK // 512, mm, 0)
        both(gbuf, in_sem.at[slot])

        if n >= 2:
            both(ggbuf, out_sem.at[slot])

        def rows(i, _):
            r = pl.ds(pl.multiple_of(i * 64, 64), 64)
            g = gbuf[slot, r, :].astype(F32)
            u = ubuf[slot, r, :].astype(F32)
            d = acc[r, :]
            s = jax.nn.sigmoid(g)
            ggbuf[slot, r, :] = (d * u * s * (1.0 + g * (1.0 - s))).astype(BF16)
            gubuf[slot, r, :] = (d * (g * s)).astype(BF16)
            return 0

        lax.fori_loop(0, TOK // 64, rows, 0)
        for cp in tile_out(n, slot):
            cp.start()
        if n + 2 < NT:
            for cp in tile_in(n + 2, slot):
                cp.start()

    tasks = dict(
        O0=O0, O1a=O1a, O1b=O1b, O2=O2, O3=O3, H=H, T=T, P=Pk, PY=PY, Z=Z, D=D,
        Wz=Wz, Wy=Wy, Wr=Wr, Wp=Wp, Wq=Wq, Wc=Wc, Ws=Ws, WD=WD,
    )
    for name, *at in SCHEDULE:
        tasks[name](*at)


def finish(norm, gg_in, gu_in, last, up_in, down_in, y_in, gg, gu, gd, total, sem):
    copies = [pltpu.make_async_copy(src, dst, sem.at[i]) for i, (src, dst) in enumerate(((gg_in, gg), (gu_in, gu)))]
    for cp in copies:
        cp.start()

    def rows(i, _):
        r = pl.ds(pl.multiple_of(i * 128, 128), 128)
        acc = last[r, :].astype(F32)
        for ref in (up_in, down_in, y_in):
            acc += ref[r, :].astype(F32)
        total[r, :] = (acc * norm).astype(BF16)
        return 0

    lax.fori_loop(0, total.shape[0] // 128, rows, 0)
    copies.append(pltpu.make_async_copy(total, gd, sem.at[2]))
    copies[-1].start()
    for cp in copies:
        cp.wait()


def shards(out_grad, gate_pre, up_pre, down_weight):
    TB, D = out_grad.shape
    TOK, FFD = gate_pre.shape
    BLK = down_weight.shape[1]
    n = len(ORDER)
    any_spec = pl.BlockSpec(memory_space=pl.ANY)
    dma = pltpu.SemaphoreType.DMA
    flops = 4 * TOK * D * FFD
    results = pl.pallas_call(
        kernel,
        out_shape=[pltpu.VMEM((TOK, FFD), BF16)] * 2 + [pltpu.VMEM((FFD, BLK), BF16)] * 4,
        in_specs=[any_spec] * 4,
        out_specs=[any_spec] * 6,
        scratch_shapes=[
            pltpu.VMEM((TOK, D), BF16),
            pltpu.VMEM((FFD, D), BF16),
            pltpu.VMEM((FFD, TOK), BF16),
            pltpu.VMEM((n, FFD, BLK), BF16),
            pltpu.VMEM((n, FFD, BLK), BF16),
            pltpu.VMEM((2, FFD, BLK), BF16),
            pltpu.VMEM((2, 2, FFD // 2, BLK), BF16),
            pltpu.VMEM((2, FFD, BLK), BF16),
            pltpu.VMEM((3, FFD - SPLIT2, BLK), BF16),
            pltpu.VMEM((TOK, BLK), F32),
            pltpu.VMEM((2, TOK, BLK), BF16),
            pltpu.VMEM((2, TOK, BLK), BF16),
            pltpu.VMEM((2, TOK, BLK), BF16),
            pltpu.VMEM((2, TOK, BLK), BF16),
            dma,
            dma,
            dma((2,)),
            dma,
            dma((n, 4)),
            dma((len(W_GROUPS),)),
            dma,
            dma((n,)),
            dma((2, 2)),
            dma((2,)),
            dma((3,)),
            dma,
            dma((2,)),
            dma,
            dma((2,)),
            dma((2,)),
            dma,
        ],
        compiler_params=pltpu.CompilerParams(
            collective_id=0, has_side_effects=True, vmem_limit_bytes=VMEM_LIMIT
        ),
        cost_estimate=pl.CostEstimate(flops=flops, bytes_accessed=40 << 20, transcendentals=0),
    )(out_grad, gate_pre, up_pre, down_weight)
    return pl.pallas_call(
        functools.partial(finish, 1.0 / math.sqrt(TOK * lax.axis_size("dp"))),
        out_shape=[jax.ShapeDtypeStruct(shape, BF16) for shape in ((TOK, FFD), (TOK, FFD), (FFD, BLK))],
        in_specs=[any_spec] * 2 + [pl.BlockSpec(memory_space=pltpu.VMEM)] * 4,
        out_specs=[any_spec] * 3,
        scratch_shapes=[pltpu.VMEM((FFD, BLK), BF16), dma((3,))],
        compiler_params=pltpu.CompilerParams(vmem_limit_bytes=2 << 20),
    )(*(pltpu.with_memory_space_constraint(a, pltpu.VMEM) for a in results))


def solution(mesh):
    return jax.shard_map(
        shards,
        mesh=mesh,
        in_specs=(P(("dp", "mp"), None), P("dp", "mp"), P("dp", "mp"), P("mp", "dp")),
        out_specs=(P("dp", "mp"), P("dp", "mp"), P("mp", "dp")),
        check_vma=False,
    )
```
